32 devices in a mesh: dp: 2 (over core), expert: 16 (over z, y, x).
Axes of the slice: x: 2, y: 2, z: 4, core: 2. Of those that a mesh axis runs over, the one named last changes fastest.
Arguments:
- tokens: bfloat16 [32768, 768], P(('dp', 'expert')), may hold values from -6 to 6
- segments: int32 [32768], P(('dp', 'expert')), may hold values from 0 to 63, never falling along the last dimension, each value on 1 to 1024 neighbouring positions
- routes: int32 [32768, 1], P(('dp', 'expert')), may hold values from 0 to 15; in each aligned block of 1024 rows (0 to 1023, 1024 to 2047, ...) at most 128 rows name the same one
- capacity: int32 [16], replicated, may hold values from 64 to 128
- first_gain: bfloat16 [768], P('dp'), may hold values from 0.5 to 1.5
- query_weight: bfloat16 [768, 768], P('dp'), may hold values from -0.21875 to 0.21875
- key_weight: bfloat16 [768, 768], P('dp'), may hold values from -0.21875 to 0.21875
- value_weight: bfloat16 [768, 768], P('dp'), may hold values from -0.21875 to 0.21875
- output_weight: bfloat16 [768, 768], P('dp'), may hold values from -1.75 to 1.75
- position_bias: bfloat16 [32, 12], P('dp'), may hold values from -3 to 3
- second_gain: bfloat16 [768], P('dp'), may hold values from 0.5 to 1.5
- router_weight: bfloat16 [768, 16], P('dp'), may hold values from -0.15625 to 0.15625
- expert_up: bfloat16 [16, 768, 3072], P('expert', None, 'dp'), may hold values from -0.21875 to 0.21875
- expert_down: bfloat16 [16, 3072, 768], P('expert', 'dp'), may hold values from -0.109375 to 0.109375
- cotangent: bfloat16 [32768, 768], P(('dp', 'expert')), may hold values from -6 to 6
Outputs:
- layer_out: bfloat16 [32768, 768], P(('dp', 'expert'))
- input_grad: bfloat16 [32768, 768], P(('dp', 'expert'))
- first_grad: float32 [768], P(('dp', 'expert'))
- query_grad: float32 [768, 768], P(('dp', 'expert'))
- key_grad: float32 [768, 768], P(('dp', 'expert'))
- value_grad: float32 [768, 768], P(('dp', 'expert'))
- output_grad: float32 [768, 768], P(('dp', 'expert'))
- bias_grad: float32 [32, 12], replicated
- second_grad: float32 [768], P(('dp', 'expert'))
- router_grad: float32 [768, 16], P(('dp', 'expert'))
- up_grad: float32 [16, 768, 3072], P('expert', None, 'dp')
- down_grad: float32 [16, 3072, 768], P('expert', 'dp')
The draws below stay inside these ranges and needn't reach their ends.
Inputs may be any that keep to these rules, and one draw needn't show every extreme that they name: `routes`: in each device's 1024 rows (an aligned block) no expert is named by more than 128 rows. `segments`: document numbers never fall along the tokens; a document has at most 1024 tokens.
All inputs are finite; a program needn't handle non-finite values.
Results may differ from the reference program's by a relative error of at most 0.014.
Values may be sent and summed in bfloat16 or wider, within the bound.
No kernel may reach another device: no remote copies, remote signals or barrier semaphores. Data moves between devices by JAX's collectives and lax.ppermute only.
A program may use at most 320 MiB of HBM per device.

```python
import math
import jax
import jax.numpy as jnp
import numpy as np
from jax import lax

D = 768
H = 12
HD = 64
FF = 3072
BUCKETS = 32
MAXDIST = 128
LENGTH = 1024
EXPERTS = 16
TOK_DEV = 1024
SEQS = 32
TOKENS = 32768
CAP = 128
DOCS = 64
N_DP = 2
N_EXPERT = 16


def draw_capacity(key, part):
    key = jax.random.fold_in(key, 7)
    spread_key, highest_key, lowest_key = jax.random.split(key, 3)
    smallest = max(1, CAP // 2)
    drawn = jax.random.randint(spread_key, (EXPERTS,), smallest, CAP + 1)
    highest = jax.random.randint(highest_key, (), 0, EXPERTS)
    lowest = (highest + 1 + jax.random.randint(lowest_key, (), 0, EXPERTS - 1)) % EXPERTS
    drawn = drawn.at[highest].set(CAP).at[lowest].set(smallest)
    return drawn.astype(jnp.int32)


def spiked(entries, own_key, source, target, blocks, factor):
    def block_of(position):
        return (jnp.arange(entries.shape[position]) // (entries.shape[position] // blocks)).reshape((-1,) + (1,) * (entries.ndim - 1 - position))

    first = jax.random.permutation(own_key, blocks)[block_of(target)]
    other_side = (block_of(target) + blocks // 2) % blocks
    return jnp.where((block_of(source) == first) | (block_of(source) == other_side), factor * entries, entries)


def block_scale(key, dims, shards, least, top_value):
    factor_of = 1.0
    for axis_at, shards_of in shards:
        heights = jax.random.uniform(jax.random.fold_in(jax.random.fold_in(key, 6), axis_at), (shards_of,), jnp.float32, least / len(shards), top_value / len(shards))
        factor_of = factor_of * jnp.repeat(jnp.exp(heights), dims[axis_at] // shards_of).reshape((-1,) + (1,) * (len(dims) - 1 - axis_at))
    return factor_of


def split_up(count, total, most, skew):
    weights = [(1 << 20) // math.isqrt(grade ** skew) + 1 for grade in range(2, count + 1)]
    rest, given = total - most - (count - 1), [1] * (count - 1)
    while rest > 0:
        candidates = [i for i in range(count - 1) if given[i] < most]
        mass, left = sum([weights[i] for i in candidates]), rest
        for i in candidates:
            more = min(most - given[i], max(1, left * weights[i] // mass), rest)
            given[i] = given[i] + more
            rest = rest - more
    return np.array([most] + given)


def uneven(rng, number_of, total, limit, lean):
    if number_of == 2:
        one = jax.random.randint(rng, (), max(1, total - limit), min(limit, total - 1) + 1)
        return jnp.stack([one, total - one])
    lengths = jnp.asarray(split_up(number_of, total, limit, lean), jnp.int32)
    twos = (number_of - 1) // 2
    source_of, taker = lengths[1:1 + 2 * twos:2], lengths[2:2 + 2 * twos:2]
    margin = jnp.minimum(source_of - 1, limit - taker)
    passed = jax.random.randint(jax.random.fold_in(rng, 1), (twos,), 0, 1 << 20) % (margin + 1)
    lengths = lengths.at[1:1 + 2 * twos:2].set(source_of - passed).at[2:2 + 2 * twos:2].set(taker + passed)
    return lengths[jax.random.permutation(jax.random.fold_in(rng, 2), number_of)]


def shared_out(own_key, own, number, rows, amount, top, bound, skew):
    ranking = jax.random.permutation(own_key, amount)
    packed, ordinary = shares(amount, rows * top, bound, skew, True), shares(amount, rows * top, bound, skew, False)
    places = jnp.arange(amount)

    def named(lengths, turn):
        used = int((lengths > 0).sum())
        fixed = max(1, used // 4)
        moved = fixed + (places - fixed + turn * (used - fixed)) % max(1, amount - fixed)
        return jnp.zeros((amount,), jnp.int32).at[ranking[jnp.where(places < fixed, places, moved)]].set(jnp.asarray(lengths, jnp.int32))

    lengths = jnp.where(number % 4 == 0, named(packed, number // 4), named(ordinary, number - number // 4 - 1))
    mixed = jax.random.permutation(jax.random.fold_in(own, 3), amount)
    donor, receiver = mixed[0:amount // 2 * 2:2], mixed[1:amount // 2 * 2:2]
    slack = jnp.minimum(lengths[donor] - 1, bound - lengths[receiver]) // 2
    slack = jnp.where((donor == ranking[0]) | (receiver == ranking[0]) | (lengths[receiver] == 0), 0, jnp.maximum(slack, 0))
    moved = jax.random.randint(jax.random.fold_in(own, 4), (amount // 2,), 0, 1 << 20) % (slack + 1)
    lengths = lengths.at[donor].add(-moved).at[receiver].add(moved)
    members = jnp.searchsorted(jnp.cumsum(lengths), jnp.arange(rows * top), side="right").astype(jnp.int32)
    grid = members.reshape(top, rows).T
    grid = grid[jax.random.permutation(jax.random.fold_in(own, 1), rows)]
    turn = jax.random.randint(jax.random.fold_in(own, 2), (rows, 1), 0, top)
    return jnp.take_along_axis(grid, (jnp.arange(top)[None, :] + turn) % top, axis=1)


def shares(number_of, total, limit, slope, full):
    portions = [(1 << 20) // math.isqrt(grade ** slope) + 1 for grade in range(1, number_of + 1)]
    largest = limit if full else min(limit, max(-(-total // number_of), total * portions[0] // sum(portions)))
    least = 1 if total - largest >= number_of - 1 else 0
    holding, surplus = [largest] + [least] * (number_of - 1), total - largest - least * (number_of - 1)
    while surplus > 0:
        free = [i for i in range(1, number_of) if holding[i] < largest] or [i for i in range(1, number_of) if holding[i] < limit]
        mass, left = sum([portions[i] for i in free]), surplus
        for i in free:
            more = min(limit - holding[i], max(1, left * portions[i] // mass), surplus)
            holding[i] = holding[i] + more
            surplus = surplus - more
    return np.array(holding)


def gaussian(own_key, shape, scale, reach, shards=(), held_as=jnp.bfloat16):
    values = scale * jax.random.normal(own_key, shape, jnp.float32)
    if shards:
        values = values * block_scale(own_key, shape, shards, -0.22, 0.18)
    return jnp.clip(values, -reach, reach).astype(held_as)


def gaussian_with(own_key, dims, width, most, cuts, heavy, kind=jnp.bfloat16):
    entries = width * jax.random.normal(own_key, dims, jnp.float32)
    if cuts:
        entries = entries * block_scale(own_key, dims, cuts, -0.22, 0.18)
    return jnp.clip(spiked(entries, jax.random.fold_in(own_key, 3), *heavy), -most, most).astype(kind)


def setup_inputs(seed: int = 0) -> dict:
    key_of = jax.random.split(jax.random.key(seed), 16)
    tokens = gaussian_with(key_of[0], (TOKENS, D), 1.0, 6.0, ((0, 32),), (0, 1, 32, 2.75))
    segments = jnp.searchsorted(jnp.cumsum(uneven(key_of[1], DOCS, TOKENS, LENGTH, 2)), jnp.arange(TOKENS), side="right").astype(jnp.int32)
    routes_keys = jax.random.split(jax.random.fold_in(key_of[2], 1), TOKENS // TOK_DEV)
    routes_turns = jax.random.permutation(jax.random.fold_in(key_of[2], 3), TOKENS // TOK_DEV)
    routes = jax.vmap(lambda own, number: shared_out(jax.random.fold_in(key_of[2], 2), own, number, TOK_DEV, EXPERTS, 1, CAP, 2))(routes_keys, routes_turns).reshape((TOKENS, 1))
    capacity = draw_capacity(jax.random.fold_in(key_of[15], 71), 0)
    first_gain = jnp.clip(1.0 + 0.1 * jax.random.normal(key_of[4], (D,), jnp.float32), 0.5, 1.5).astype(jnp.bfloat16)
    query_weight = gaussian(key_of[5], (D, D), D ** -0.5, 0.21875, ((0, 2),))
    key_weight = gaussian(key_of[6], (D, D), D ** -0.5, 0.21875, ((0, 2),))
    value_weight = gaussian(key_of[7], (D, D), D ** -0.5, 0.21875, ((0, 2),))
    output_weight = gaussian(key_of[8], (D, D), (D // 64) ** -0.5, 1.75, ((0, 2),))
    position_bias = gaussian(key_of[9], (BUCKETS, H), 0.5, 3.0, ((0, 2),))
    second_gain = jnp.clip(1.0 + 0.1 * jax.random.normal(key_of[10], (D,), jnp.float32), 0.5, 1.5).astype(jnp.bfloat16)
    router_weight = gaussian(key_of[11], (D, EXPERTS), (2 * D) ** -0.5, 0.15625, ((0, 2),))
    expert_up = gaussian(key_of[12], (EXPERTS, D, FF), D ** -0.5, 0.21875, ((0, 16), (2, 2)))
    expert_down = gaussian(key_of[13], (EXPERTS, FF, D), FF ** -0.5, 0.109375, ((0, 16), (1, 2)))
    cotangent = gaussian(key_of[14], (TOKENS, D), 1.0, 6.0, ((0, 32),))
    return dict(tokens=tokens, segments=segments, routes=routes, capacity=capacity, first_gain=first_gain, query_weight=query_weight, key_weight=key_weight, value_weight=value_weight, output_weight=output_weight, position_bias=position_bias, second_gain=second_gain, router_weight=router_weight, expert_up=expert_up, expert_down=expert_down, cotangent=cotangent)


@jax.custom_vjp
def low(v):
    return lax.optimization_barrier(v.astype(jnp.bfloat16)).astype(jnp.float32)

@jax.custom_vjp
def low_back(v):
    return v

def low_keep(v):
    return (low(v), None)

def low_pass(kept, grad):
    return (grad,)

def back_keep(v):
    return (v, None)

def back_low(kept, grad):
    return (low(grad),)
low.defvjp(low_keep, low_pass)
low_back.defvjp(back_keep, back_low)
epsilon = 1e-06
highest = lax.Precision.HIGHEST

def bucket_table(length, buckets, max_reach):
    offsets = np.arange(-(length - 1), length)
    halved = buckets // 2
    linear = halved // 2
    upward = (offsets > 0).astype(np.int64) * halved
    distance = np.abs(offsets)
    scaled = np.log(np.maximum(distance, 1) / linear) / np.log(max_reach / linear) * (halved - linear)
    logpart = np.minimum(linear + np.floor(np.maximum(scaled, 0.0)).astype(np.int64), halved - 1)
    return (upward + np.where(distance < linear, distance, logpart)).astype(np.int32)

def bucket_matrix(length, buckets, max_reach):
    lookup = bucket_table(length, buckets, max_reach)
    across = np.arange(length)
    return lookup[across[None, :] - across[:, None] + length - 1]

def rms_norm(values, gain):
    return values * lax.rsqrt(lax.optimization_barrier(jnp.mean(values * values, axis=-1, keepdims=True)) + epsilon) * gain

def gate_values(logits, chosen):
    probability = jax.nn.softmax(logits, axis=-1)
    return logits.shape[-1] * lax.optimization_barrier(jnp.sum(jnp.where(chosen, probability, 0.0), axis=-1))

def reference(tokens, segments, routes, capacity, first_gain, query_weight, key_weight, value_weight, output_weight, position_bias, second_gain, router_weight, expert_up, expert_down, cotangent):
    devices_all = N_DP * N_EXPERT
    bucket_ids = jnp.asarray(bucket_matrix(LENGTH, BUCKETS, MAXDIST))
    scale_factor = HD ** (-0.5)
    chosen_expert = routes[:, 0]
    chosen = chosen_expert[:, None] == jnp.arange(EXPERTS, dtype=jnp.int32)[None, :]
    blocked = chosen.reshape(devices_all, TOK_DEV, EXPERTS).astype(jnp.int32)
    places = lax.optimization_barrier(jnp.sum((jnp.cumsum(blocked, axis=1) - 1) * blocked, axis=-1)).reshape(TOKENS)
    limits = lax.optimization_barrier(jnp.sum(jnp.where(chosen, capacity[None, :], 0), axis=-1))
    kept = places < limits
    places = jnp.where(kept, places, CAP).astype(jnp.int32)
    owner_device = (jnp.arange(TOKENS, dtype=jnp.int32) // TOK_DEV).astype(jnp.int32)
    segment_seqs = segments.reshape(SEQS, LENGTH)

    def forward(inputs, first_f, query_f, key_f, value_f, output_f, bias_f, second_f, router_f, up_f, down_f):
        normed = low(rms_norm(inputs, first_f))
        queries = low_back(low(jnp.dot(normed, query_f, precision=highest)))
        keys_all = low_back(low(jnp.dot(normed, key_f, precision=highest)))
        values_all = low_back(low(jnp.dot(normed, value_f, precision=highest)))

        def one_sequence(pieces):
            query_seq, key_seq, value_seq, segment_seq = pieces
            relative = bias_f[bucket_ids].transpose(2, 0, 1)
            query_heads = query_seq.reshape(LENGTH, H, HD)
            key_heads = key_seq.reshape(LENGTH, H, HD)
            value_heads = value_seq.reshape(LENGTH, H, HD)
            scores = jnp.einsum('qhd,khd->hqk', query_heads, key_heads, precision=highest) * scale_factor + relative
            same_doc = segment_seq[:, None] == segment_seq[None, :]
            scores = low_back(jnp.where(same_doc[None], scores, -1e+30))
            weights = low(jax.nn.softmax(scores, axis=-1))
            return jnp.einsum('hqk,khd->qhd', weights, value_heads, precision=highest).reshape(LENGTH, D)
        attended = lax.map(jax.checkpoint(one_sequence), (queries.reshape(SEQS, LENGTH, D), keys_all.reshape(SEQS, LENGTH, D), values_all.reshape(SEQS, LENGTH, D), segment_seqs))
        heads = low_back(low(attended.reshape(TOKENS, D)))
        branch = low_back(jnp.dot(heads, output_f, precision=highest))
        hidden = inputs + branch
        normed_ffn = low(rms_norm(hidden, second_f))
        logits = low_back(jnp.dot(normed_ffn, router_f, precision=highest))
        gates = gate_values(logits, chosen)
        slots = jnp.zeros((EXPERTS, devices_all, CAP + 1, D), jnp.float32).at[chosen_expert, owner_device, places].set(normed_ffn)
        dispatched = low_back(slots[:, :, :CAP].reshape(EXPERTS, devices_all * CAP, D))

        def one_expert(pieces):
            expert_rows, up_matrix, down_matrix = pieces
            before = low_back(jnp.dot(expert_rows, up_matrix, precision=highest))
            activated = low(jax.nn.gelu(before, approximate=True))
            return low_back(low(jnp.dot(activated, down_matrix, precision=highest)))
        produced = lax.map(jax.checkpoint(one_expert), (dispatched, up_f, down_f)).reshape(EXPERTS, devices_all, CAP, D)
        returned = produced[chosen_expert, owner_device, jnp.minimum(places, CAP - 1)]
        returned = jnp.where(kept[:, None], returned, 0.0)
        return hidden + gates[:, None] * returned
    floats = (tokens.astype(jnp.float32), first_gain.astype(jnp.float32), query_weight.astype(jnp.float32), key_weight.astype(jnp.float32), value_weight.astype(jnp.float32), output_weight.astype(jnp.float32), position_bias.astype(jnp.float32), second_gain.astype(jnp.float32), router_weight.astype(jnp.float32), expert_up.astype(jnp.float32), expert_down.astype(jnp.float32))
    result, pullback = jax.vjp(forward, *floats)
    grads = pullback(cotangent.astype(jnp.float32))
    return (result.astype(jnp.bfloat16), grads[0].astype(jnp.bfloat16), grads[1], grads[2], grads[3], grads[4], grads[5], grads[6], grads[7], grads[8], grads[9], grads[10])
```

```python
from functools import partial

import jax
import jax.numpy as jnp
import numpy as np
from jax import lax
from jax.experimental import pallas as pl
from jax.experimental.pallas import tpu as pltpu
from jax.sharding import PartitionSpec as P

D = 768
H = 12
HD = 64
BUCKETS = 32
MAXDIST = 128
LENGTH = 1024
TILE = 128
REACH = 512
LANES = 128
epsilon = 1e-06
VMEM_LIMIT = 56 * 2**20

bf16 = jnp.bfloat16
f32 = jnp.float32
NN = (((1,), (0,)), ((), ()))
NT = (((1,), (1,)), ((), ()))
TN = (((0,), (0,)), ((), ()))


def dot(left, right, dims=NN):
    return lax.dot_general(left, right, dims, preferred_element_type=f32)


def bucket_table(length, buckets, max_reach):
    offsets = np.arange(-(length - 1), length)
    halved = buckets // 2
    linear = halved // 2
    upward = (offsets > 0).astype(np.int64) * halved
    distance = np.abs(offsets)
    scaled = (
        np.log(np.maximum(distance, 1) / linear) / np.log(max_reach / linear) * (halved - linear)
    )
    logpart = np.minimum(linear + np.floor(np.maximum(scaled, 0.0)).astype(np.int64), halved - 1)
    return (upward + np.where(distance < linear, distance, logpart)).astype(np.int32)


def bucket_onehot(offsets):
    table = bucket_table(LENGTH, BUCKETS, MAXDIST)
    return (table[offsets + LENGTH - 1][:, None] == np.arange(BUCKETS)[None, :]).astype(np.float32)


def forward_kernel(bias_ref, rows_ref, cols_ref, q_ref, k_ref, v_ref, o_ref, e_ref, r_ref, w_ref):
    low = lax.broadcasted_iota(jnp.int32, (1, LANES), 1) < HD
    blocks = LENGTH // TILE
    count = LENGTH // 2
    edge = LENGTH - 2 * TILE
    k = k_ref[...]
    v = v_ref[...]
    cols = cols_ref[...]
    for hh in range(2):
        own = low if hh == 0 else ~low
        near = bias_ref[0, hh : hh + 1, :]
        middle = pltpu.roll(
            jnp.broadcast_to(near, (TILE, REACH)), REACH - TILE, axis=1, stride=1, stride_axis=0
        )
        w_ref[:, :edge] = jnp.broadcast_to(near[:, :1], (TILE, edge))
        w_ref[:, edge : edge + 3 * TILE] = middle[:, : 3 * TILE]
        w_ref[:, edge + 3 * TILE :] = jnp.broadcast_to(near[:, REACH - 1 :], (TILE, edge))
        key = jnp.where(own, k, jnp.zeros_like(k))
        value = jnp.where(own, v, jnp.ones_like(v))
        for base in range(0, LENGTH, count):
            here = slice(base, base + count)
            starts = [TILE * (blocks - 1 - a) for a in range(base // TILE, (base + count) // TILE)]
            bias = jnp.concatenate([w_ref[:, s : s + LENGTH] for s in starts], axis=0)
            scores = dot(q_ref[here], key, NT) + bias
            scores = jnp.where(rows_ref[here] == cols, scores, -1e30)
            largest = jnp.max(scores, axis=1, keepdims=True)
            shifted = jnp.exp(scores - largest).astype(bf16)
            e_ref[hh, here, :] = shifted
            summed = dot(shifted, value)
            inverse = 1.0 / pltpu.roll(summed, HD, axis=1)
            result = (summed * inverse).astype(bf16)
            if hh == 0:
                o_ref[here] = result
                r_ref[here] = inverse
            else:
                o_ref[here] = jnp.where(low, o_ref[here], result)
                r_ref[here] = jnp.where(low, r_ref[here], inverse)


def attend(bias, rows, cols, qkv):
    pairs = D // LANES
    part = lambda at: pl.BlockSpec((LENGTH, LANES), lambda p, at=at: (0, at * pairs + p))
    return pl.pallas_call(
        forward_kernel,
        grid=(pairs,),
        in_specs=[
            pl.BlockSpec((1, 2, REACH), lambda p: (p, 0, 0)),
            pl.BlockSpec((LENGTH, 1), lambda p: (0, 0)),
            pl.BlockSpec((1, LENGTH), lambda p: (0, 0)),
            part(0),
            part(1),
            part(2),
        ],
        out_specs=[
            part(0),
            pl.BlockSpec((2, LENGTH, LENGTH), lambda p: (p, 0, 0)),
            part(0),
        ],
        out_shape=[
            jax.ShapeDtypeStruct((LENGTH, D), bf16),
            jax.ShapeDtypeStruct((H, LENGTH, LENGTH), bf16),
            jax.ShapeDtypeStruct((LENGTH, D), f32),
        ],
        scratch_shapes=[pltpu.VMEM((TILE, 2 * LENGTH - TILE), f32)],
        compiler_params=pltpu.CompilerParams(vmem_limit_bytes=VMEM_LIMIT),
        cost_estimate=pl.CostEstimate(
            flops=16 * H * LENGTH * LENGTH * HD,
            bytes_accessed=40 * 2**20,
            transcendentals=H * LENGTH * LENGTH,
        ),
        name="attend",
    )(bias, rows, cols, qkv, qkv, qkv)


def backward_kernel(
    q_ref, k_ref, v_ref, g_ref, o_ref, r_ref, e_ref, dq_ref, dk_ref, dv_ref, near_ref, t_ref
):
    lane = lax.broadcasted_iota(jnp.int32, (1, LANES), 1)
    low = lane < HD
    blocks = LENGTH // TILE
    block_of = lax.broadcasted_iota(jnp.int32, (LENGTH, LANES), 0) // TILE
    lanes = lax.broadcasted_iota(jnp.int32, (LENGTH, LANES), 1)
    q = q_ref[...]
    k = k_ref[...]
    v = v_ref[...]
    for hh in range(2):
        own = low if hh == 0 else ~low
        free = HD * (1 - hh)
        key = jnp.where(own, k, (lanes - free == block_of).astype(bf16))
        ones = jnp.where((lane == free) | (lane == free + 1), 1.0, 0.0).astype(bf16)
        value = jnp.where(own, v, ones)
        grad = jnp.where(own, g_ref[...].astype(f32) * r_ref[...], 0.0)
        term = -jnp.sum(grad * o_ref[...].astype(f32), axis=1, keepdims=True)
        grad = grad.astype(bf16)
        high = term.astype(bf16)
        rest = (term - high.astype(f32)).astype(bf16)
        joined = jnp.where(lane == free, high, jnp.where(lane == free + 1, rest, grad))
        shifted = e_ref[hh]
        ds = shifted * dot(joined, value, NT).astype(bf16)
        dq = dot(ds, key)
        t_ref[...] = jnp.zeros_like(t_ref)
        leftward = jnp.zeros((1, LANES), f32)
        rightward = jnp.zeros((1, LANES), f32)
        for a in range(blocks):
            first, last = max(a - 1, 0), min(a + 2, blocks)
            at = slice(a * TILE, (a + 1) * TILE)
            to = slice(TILE * (first - a + 1), TILE * (last - a + 1))
            t_ref[:, to] += ds[at, TILE * first : TILE * last].astype(f32)
            totals = jnp.sum(dq[at], axis=0, keepdims=True)
            block = lane - free
            leftward += jnp.where((block >= 0) & (block <= a - 2), totals, 0.0)
            rightward += jnp.where((block >= a + 2) & (block < blocks), totals, 0.0)
        dq = (dq * HD ** (-0.5)).astype(bf16)
        dv = dot(grad, shifted, TN).T.astype(bf16)
        dk = dot(q, ds, TN).T.astype(bf16)
        if hh == 0:
            dq_ref[...] = dq
            dk_ref[...] = dk
            dv_ref[...] = dv
        else:
            dq_ref[...] = jnp.where(low, dq_ref[...], dq)
            dk_ref[...] = jnp.where(low, dk_ref[...], dk)
            dv_ref[...] = jnp.where(low, dv_ref[...], dv)
        diagonals = jnp.concatenate([t_ref[...], jnp.zeros((TILE, TILE), f32)], axis=1)
        row = lax.broadcasted_iota(jnp.int32, (TILE, REACH), 0)
        for bit in range(7):
            moved = pltpu.roll(diagonals, REACH - (1 << bit), axis=1)
            diagonals = jnp.where(((row >> bit) & 1) == 1, moved, diagonals)
        at = lax.broadcasted_iota(jnp.int32, (1, REACH), 1)
        near_ref[0, hh : hh + 1, :] = (
            jnp.sum(diagonals, axis=0, keepdims=True)
            + jnp.where(at == 3 * TILE + 16, jnp.sum(leftward, axis=1, keepdims=True), 0.0)
            + jnp.where(at == 3 * TILE - 1, jnp.sum(rightward, axis=1, keepdims=True), 0.0)
        )


def attend_back(qkv, grad, heads, inverse, shifted, first, pairs):
    every = D // LANES
    part = lambda at: pl.BlockSpec((LENGTH, LANES), lambda p, at=at: (0, at * every + first + p))
    out = pl.BlockSpec((LENGTH, LANES), lambda p: (0, p))
    return pl.pallas_call(
        backward_kernel,
        grid=(pairs,),
        in_specs=[part(0), part(1), part(2), part(0), part(0), part(0)]
        + [pl.BlockSpec((2, LENGTH, LENGTH), lambda p: (first + p, 0, 0))],
        out_specs=[out, out, out]
        + [pl.BlockSpec((1, 2, REACH), lambda p: (p, 0, 0))],
        out_shape=[jax.ShapeDtypeStruct((LENGTH, pairs * LANES), bf16)] * 3
        + [jax.ShapeDtypeStruct((pairs, 2, REACH), f32)],
        scratch_shapes=[pltpu.VMEM((TILE, 3 * TILE), f32)],
        compiler_params=pltpu.CompilerParams(vmem_limit_bytes=VMEM_LIMIT),
        cost_estimate=pl.CostEstimate(
            flops=64 * pairs * LENGTH * LENGTH * HD,
            bytes_accessed=pairs * 6 * 2**20,
            transcendentals=0,
        ),
        name="attend_back",
    )(qkv, qkv, qkv, grad, heads, inverse, shifted)


def expert_kernel(
    me_ref, rows_ref, cot_ref, router_ref, up0_ref, up1_ref, down0_ref, down1_ref,
    sent_ref, back_ref, gp_ref, gl_ref, act_ref, gb_ref,
    out_ref, grow_ref, p_ref, gate_ref, *, experts, steps,
):
    step = pl.program_id(0)
    me = me_ref[0]
    lane = lax.broadcasted_iota(jnp.int32, (1, LANES), 1)

    @pl.when(step == 0)
    def _():
        logits = dot(rows_ref[...], router_ref[...])
        logits = jnp.where(lane < experts, logits, -1e30)
        weight = jnp.exp(logits - jnp.max(logits, axis=1, keepdims=True))
        p = weight / jnp.sum(weight, axis=1, keepdims=True)
        gate = experts * jnp.sum(jnp.where(lane == me, p, 0.0), axis=1, keepdims=True)
        p_ref[...] = p
        gate_ref[...] = gate
        gp_ref[...] = (gate * cot_ref[...].astype(f32)).astype(bf16)
        out_ref[...] = jnp.zeros_like(out_ref)
        grow_ref[...] = jnp.zeros_like(grow_ref)

    mine = step < steps // 2
    up = jnp.where(mine, up0_ref[...], up1_ref[...])
    down = jnp.where(mine, down0_ref[...], down1_ref[...])
    v = dot(rows_ref[...], up)
    scale = np.sqrt(2 / np.pi).astype(np.float32)
    square = v * v
    tanh = jnp.tanh(scale * v * (1.0 + 0.044715 * square))
    half = 0.5 + 0.5 * tanh
    act = (v * half).astype(bf16)
    slope = half + (0.5 * scale) * v * (1.0 - tanh * tanh) * (1.0 + (3 * 0.044715) * square)
    gb = (slope * dot(gp_ref[...], down, NT)).astype(bf16)
    act_ref[0] = act
    gb_ref[0] = gb
    out_ref[...] += dot(act, down)
    grow_ref[...] += dot(gb, up, NT)

    @pl.when(step == steps - 1)
    def _():
        gate = gate_ref[...]
        produced = out_ref[...]
        sent_ref[...] = (gate * produced).astype(bf16)
        grad_gate = jnp.sum(produced * cot_ref[...].astype(f32), axis=1, keepdims=True)
        chosen = jnp.where(lane == me, 1.0, 0.0)
        grad_logits = (grad_gate * gate * (chosen - p_ref[...])).astype(bf16)
        gl_ref[...] = grad_logits
        back_ref[...] = (grow_ref[...] + dot(grad_logits, router_ref[...], NT)).astype(bf16)


def expert_part(me, rows, cot, router, up0, up1, down0, down1, experts):
    count = rows.shape[0]
    half = up0.shape[1]
    tile = 512
    each = half // tile
    steps = 2 * each
    whole = pl.BlockSpec((count, D), lambda f: (0, 0))
    narrow = pl.BlockSpec((count, LANES), lambda f: (0, 0))
    near = lambda f: jnp.minimum(f, each - 1)
    later = lambda f: jnp.maximum(f - each, 0)
    wide = pl.BlockSpec((1, count, tile), lambda f: (f // each, 0, f % each))
    return pl.pallas_call(
        partial(expert_kernel, experts=experts, steps=steps),
        grid=(steps,),
        in_specs=[
            pl.BlockSpec(memory_space=pltpu.SMEM),
            whole,
            whole,
            pl.BlockSpec((D, LANES), lambda f: (0, 0)),
            pl.BlockSpec((D, tile), lambda f: (0, near(f))),
            pl.BlockSpec((D, tile), lambda f: (0, later(f))),
            pl.BlockSpec((tile, D), lambda f: (near(f), 0)),
            pl.BlockSpec((tile, D), lambda f: (later(f), 0)),
        ],
        out_specs=[whole, whole, whole, narrow, wide, wide],
        out_shape=[
            jax.ShapeDtypeStruct((count, D), bf16),
            jax.ShapeDtypeStruct((count, D), bf16),
            jax.ShapeDtypeStruct((count, D), bf16),
            jax.ShapeDtypeStruct((count, LANES), bf16),
            jax.ShapeDtypeStruct((2, count, half), bf16),
            jax.ShapeDtypeStruct((2, count, half), bf16),
        ],
        scratch_shapes=[
            pltpu.VMEM((count, D), f32),
            pltpu.VMEM((count, D), f32),
            pltpu.VMEM((count, LANES), f32),
            pltpu.VMEM((count, 1), f32),
        ],
        compiler_params=pltpu.CompilerParams(vmem_limit_bytes=VMEM_LIMIT),
        cost_estimate=pl.CostEstimate(
            flops=16 * count * D * half,
            bytes_accessed=30 * 2**20,
            transcendentals=2 * count * half,
        ),
        name="expert_part",
    )(me, rows, cot, router, up0, up1, down0, down1)


def shards(
    tokens,
    segments,
    routes,
    capacity,
    first_gain,
    query_weight,
    key_weight,
    value_weight,
    output_weight,
    position_bias,
    second_gain,
    router_weight,
    expert_up,
    expert_down,
    cotangent,
):
    owners = lax.axis_size("expert")
    cores = lax.axis_size("dp")
    core = lax.axis_index("dp")
    expert = lax.axis_index("expert")
    token_count = tokens.shape[0]
    experts = capacity.shape[0]
    slots = 2 * token_count // experts
    chunk = slots // 2
    swap = [(i, i ^ 1) for i in range(cores)]
    inner = 1 << ((owners.bit_length() - 1) // 2)
    outer = owners // inner
    inner_groups = [[o * inner + i for i in range(inner)] for o in range(outer)]
    outer_groups = [[o * inner + i for o in range(outer)] for i in range(inner)]
    share = D // cores // owners

    def other_core(value):
        return lax.ppermute(value, "dp", swap)

    def both(mine, other):
        return jnp.where(
            core == 0,
            jnp.concatenate([mine, other], axis=0),
            jnp.concatenate([other, mine], axis=0),
        )

    def exchange(value):
        shape = (experts, chunk, D)
        return lax.all_to_all(
            value.reshape(shape), "expert", split_axis=0, concat_axis=0, tiled=True
        ).reshape(experts * chunk, D)

    choice = routes.reshape(1, token_count)
    chosen = choice == lax.broadcasted_iota(jnp.int32, (experts, token_count), 0)
    before = (
        lax.broadcasted_iota(jnp.int32, (token_count, token_count), 0)
        < lax.broadcasted_iota(jnp.int32, (token_count, token_count), 1)
    ).astype(bf16)
    earlier = dot(chosen.astype(bf16), before)
    place = jnp.sum(jnp.where(chosen, earlier, 0.0), axis=0, keepdims=True).astype(jnp.int32)
    limit = jnp.sum(jnp.where(chosen, capacity[:, None], 0), axis=0, keepdims=True)
    kept = place < limit
    slot = choice * chunk + place % chunk
    slot_ids = lax.broadcasted_iota(jnp.int32, (experts * chunk, token_count), 0)
    picks = [
        (jnp.where(kept & (place // chunk == c), slot, -1) == slot_ids).astype(bf16)
        for c in range(2)
    ]
    picks = lax.optimization_barrier(picks)
    cot_sent = [dot(pick, cotangent).astype(bf16) for pick in picks]
    cot_rows = [exchange(rows) for rows in cot_sent]

    small = jnp.concatenate(
        [
            router_weight,
            first_gain[:, None],
            second_gain[:, None],
            jnp.zeros((D // cores, LANES - 2), bf16),
        ],
        axis=1,
    )
    mixer = jnp.concatenate([query_weight, key_weight, value_weight, output_weight], axis=1)
    mixer_full = both(mixer, other_core(mixer))
    small_full = both(small, other_core(small))
    bias_full = both(position_bias, other_core(position_bias)).astype(f32)
    up0 = expert_up[0]
    down0 = expert_down[0]
    up1 = other_core(up0)
    down1 = other_core(down0)
    router = small_full[:, :experts]
    gains = small_full[:, experts : experts + 2].astype(f32).T
    first_full = gains[0:1]
    second_full = gains[1:2]
    router_wide = jnp.pad(router, ((0, 0), (0, LANES - experts)))
    qkv_full = mixer_full[:, : 3 * D]
    output_full = mixer_full[:, 3 * D :]

    inputs = tokens.astype(f32)
    first_scale = lax.rsqrt(jnp.mean(inputs * inputs, axis=-1, keepdims=True) + epsilon)
    attn_low = (inputs * first_scale * first_full).astype(bf16)
    scaling = np.where(np.arange(3 * D) < D, HD ** (-0.5), 1.0).astype(np.float32)
    qkv = (dot(attn_low, qkv_full) * scaling[None, :]).astype(bf16)
    near = np.clip(np.arange(REACH) - REACH // 2, 1 - LENGTH, LENGTH - 1)
    bias = jnp.dot(jnp.asarray(bucket_onehot(near)), bias_full, precision=lax.Precision.HIGHEST)
    bias = bias.T.reshape(H // 2, 2, REACH)
    marks = segments.astype(f32)
    heads_low, shifted, inverse = attend(bias, marks[:, None], marks[None, :], qkv)
    hidden = inputs + dot(heads_low, output_full)
    second_scale = lax.rsqrt(jnp.mean(hidden * hidden, axis=-1, keepdims=True) + epsilon)
    ffn_low = (hidden * second_scale * second_full).astype(bf16)

    me = expert.reshape(1).astype(jnp.int32)
    ffn_low, *cot_rows = lax.optimization_barrier((ffn_low, *cot_rows))
    sent = [dot(pick, ffn_low).astype(bf16) for pick in picks]
    rows0 = exchange(sent[0])
    sent1, rows0 = lax.optimization_barrier((sent[1], rows0))
    rows1 = exchange(sent1)
    arrived = [rows0, rows1]
    parts = [
        expert_part(me, arrived[c], cot_rows[c], router_wide, up0, up1, down0, down1, experts)
        for c in range(2)
    ]
    back0 = exchange(parts[0][1])
    back_sent1, back0 = lax.optimization_barrier((parts[1][1], back0))
    back1 = exchange(back_sent1)

    def summed(left, right):
        return dot(left[0], right[0], TN) + dot(left[1], right[1], TN)

    def of_half(at, half):
        return [part[at][half] for part in parts]

    gps = [part[2] for part in parts]
    down_sent = summed(of_half(4, 1), gps).astype(bf16)
    up_sent = summed(arrived, of_half(5, 1)).astype(bf16)
    down_grad = summed(of_half(4, 0), gps) + other_core(down_sent).astype(f32)
    up_grad = summed(arrived, of_half(5, 0)) + other_core(up_sent).astype(f32)
    router_term = summed(arrived, [part[3] for part in parts])[:, :experts]

    grad_out = cotangent.astype(f32)
    grad_ffn = summed(picks, [back0, back1])
    weighted = second_full * grad_ffn
    second_term = jnp.sum(grad_ffn * hidden * second_scale, axis=0, keepdims=True)
    grad_hidden = (
        grad_out
        + second_scale * weighted
        - hidden * second_scale**3 * jnp.mean(weighted * hidden, axis=-1, keepdims=True)
    )
    grad_branch = grad_hidden.astype(bf16)
    grad_heads = dot(grad_branch, output_full, NT).astype(bf16)

    out_sent0, out_sent1, grad_heads = lax.optimization_barrier(
        (parts[0][0], parts[1][0], grad_heads)
    )
    out0 = exchange(out_sent0)
    out1 = exchange(out_sent1)
    dq, dk, dv, near_sums = attend_back(
        qkv, grad_heads, heads_low, inverse, shifted, 0, H // 2
    )
    layer_out = (hidden + summed(picks, [out0, out1])).astype(bf16)

    offsets = np.arange(REACH)
    offsets = np.where(offsets < 3 * TILE, offsets - TILE, offsets - TILE - REACH)
    bias_term = jnp.dot(
        jnp.asarray(bucket_onehot(offsets).T),
        near_sums.reshape(H, REACH).T,
        precision=lax.Precision.HIGHEST,
    )

    weights = [qkv_full[:, at * D : (at + 1) * D] for at in range(3)]
    grads = [dq, dk, dv]
    grad_attn = sum(dot(g, w, NT) for g, w in zip(grads, weights))
    weighted = first_full * grad_attn
    first_term = jnp.sum(grad_attn * inputs * first_scale, axis=0, keepdims=True)
    input_grad = (
        grad_hidden
        + first_scale * weighted
        - inputs * first_scale**3 * jnp.mean(weighted * inputs, axis=-1, keepdims=True)
    ).astype(bf16)

    order = np.arange(D).reshape(cores, outer, inner, share).transpose(0, 2, 1, 3).reshape(cores, -1)
    orders = jnp.where(core == 0, order, order[::-1])
    selector = (jnp.arange(D)[:, None, None] == orders[None]).astype(bf16)

    def halves(value):
        return [dot(value, selector[:, at]).astype(bf16) for at in range(2)]

    attn_halves = halves(attn_low)
    head_halves = halves(heads_low)

    def spread(terms, extra):
        columns = terms.shape[1]
        extra_sent = jnp.broadcast_to(extra[None], (owners,) + extra.shape)
        terms = terms.reshape(owners, share, columns)
        return jnp.concatenate([terms, extra_sent], axis=1)

    def pieces(half):
        others = [
            router_term.reshape(cores, -1, experts),
            second_term.reshape(cores, -1, 1),
            first_term.reshape(cores, -1, 1),
        ]
        others = jnp.concatenate(others, axis=2).reshape(cores, outer, inner, share, experts + 2)
        others = others.transpose(0, 2, 1, 3, 4).reshape(cores, -1, experts + 2)
        others = jnp.where((core == 0) == (half == 0), others[0], others[1])
        wide = [dot(attn_halves[half], g, TN) for g in grads]
        wide.append(dot(head_halves[half], grad_branch, TN))
        joined = jnp.concatenate(wide + [others], axis=1)
        return jnp.pad(joined, ((0, 0), (0, -joined.shape[1] % LANES)))

    columns = 4 * D + experts + 2
    columns = columns + -columns % LANES
    bias_row = jnp.pad(bias_term.reshape(1, BUCKETS * H), ((0, 0), (0, columns - BUCKETS * H)))
    other_half = jnp.concatenate([pieces(1), bias_row], axis=0).astype(bf16)
    sums = jnp.concatenate([pieces(0), bias_row], axis=0) + other_core(other_half).astype(f32)
    sums = spread(sums[:-1], sums[-1:]).astype(bf16)
    width = outer * (share + 1)
    sums = lax.all_to_all(
        sums.reshape(inner, width, columns),
        "expert",
        split_axis=0,
        concat_axis=0,
        tiled=True,
        axis_index_groups=inner_groups,
    )
    sums = jnp.sum(sums.astype(f32), axis=0).astype(bf16)
    sums = lax.all_to_all(
        sums.reshape(outer, share + 1, columns),
        "expert",
        split_axis=0,
        concat_axis=0,
        tiled=True,
        axis_index_groups=outer_groups,
    )
    sums = jnp.sum(sums.astype(f32), axis=0)
    bias_grad = sums[share, : BUCKETS * H].reshape(BUCKETS, H)
    sums = sums[:share]
    query_grad, key_grad, value_grad, output_grad = [
        sums[:, at * D : (at + 1) * D] for at in range(4)
    ]
    router_grad = sums[:, 4 * D : 4 * D + experts]
    second_grad = sums[:, 4 * D + experts]
    first_grad = sums[:, 4 * D + experts + 1]
    return (
        layer_out,
        input_grad,
        first_grad,
        query_grad,
        key_grad,
        value_grad,
        output_grad,
        bias_grad,
        second_grad,
        router_grad,
        up_grad[None],
        down_grad[None],
    )


def solution(mesh):
    both = ("dp", "expert")
    placed = (
        P(both, None),
        P(both),
        P(both, None),
        P(),
        P("dp"),
        P("dp", None),
        P("dp", None),
        P("dp", None),
        P("dp", None),
        P("dp", None),
        P("dp"),
        P("dp", None),
        P("expert", None, "dp"),
        P("expert", "dp", None),
        P(both, None),
    )
    return jax.shard_map(
        shards,
        mesh=mesh,
        in_specs=placed,
        out_specs=(
            P(both, None),
            P(both, None),
            P(both),
            P(both, None),
            P(both, None),
            P(both, None),
            P(both, None),
            P(),
            P(both),
            P(both, None),
            P("expert", None, "dp"),
            P("expert", "dp", None),
        ),
        check_vma=False,
    )
```

```python
from functools import partial

import jax
import jax.numpy as jnp
import numpy as np
from jax import lax
from jax.experimental import pallas as pl
from jax.experimental.pallas import tpu as pltpu
from jax.sharding import PartitionSpec as P

D = 768
H = 12
HD = 64
BUCKETS = 32
MAXDIST = 128
LENGTH = 1024
TILE = 128
REACH = 512
LANES = 128
epsilon = 1e-06
VMEM_LIMIT = 56 * 2**20

bf16 = jnp.bfloat16
f32 = jnp.float32
NN = (((1,), (0,)), ((), ()))
NT = (((1,), (1,)), ((), ()))
TN = (((0,), (0,)), ((), ()))


def dot(left, right, dims=NN):
    return lax.dot_general(left, right, dims, preferred_element_type=f32)


def bucket_table(length, buckets, max_reach):
    offsets = np.arange(-(length - 1), length)
    halved = buckets // 2
    linear = halved // 2
    upward = (offsets > 0).astype(np.int64) * halved
    distance = np.abs(offsets)
    scaled = (
        np.log(np.maximum(distance, 1) / linear) / np.log(max_reach / linear) * (halved - linear)
    )
    logpart = np.minimum(linear + np.floor(np.maximum(scaled, 0.0)).astype(np.int64), halved - 1)
    return (upward + np.where(distance < linear, distance, logpart)).astype(np.int32)


def bucket_onehot(offsets):
    table = bucket_table(LENGTH, BUCKETS, MAXDIST)
    return (table[offsets + LENGTH - 1][:, None] == np.arange(BUCKETS)[None, :]).astype(np.float32)


def forward_kernel(bias_ref, rows_ref, cols_ref, q_ref, k_ref, v_ref, o_ref, e_ref, r_ref, w_ref):
    low = lax.broadcasted_iota(jnp.int32, (1, LANES), 1) < HD
    blocks = LENGTH // TILE
    count = LENGTH // 2
    edge = LENGTH - 2 * TILE
    k = k_ref[...]
    v = v_ref[...]
    cols = cols_ref[...]
    for hh in range(2):
        own = low if hh == 0 else ~low
        near = bias_ref[0, hh : hh + 1, :]
        middle = pltpu.roll(
            jnp.broadcast_to(near, (TILE, REACH)), REACH - TILE, axis=1, stride=1, stride_axis=0
        )
        w_ref[:, :edge] = jnp.broadcast_to(near[:, :1], (TILE, edge))
        w_ref[:, edge : edge + 3 * TILE] = middle[:, : 3 * TILE]
        w_ref[:, edge + 3 * TILE :] = jnp.broadcast_to(near[:, REACH - 1 :], (TILE, edge))
        key = jnp.where(own, k, jnp.zeros_like(k))
        value = jnp.where(own, v, jnp.ones_like(v))
        for base in range(0, LENGTH, count):
            here = slice(base, base + count)
            starts = [TILE * (blocks - 1 - a) for a in range(base // TILE, (base + count) // TILE)]
            bias = jnp.concatenate([w_ref[:, s : s + LENGTH] for s in starts], axis=0)
            scores = dot(q_ref[here], key, NT) + bias
            scores = jnp.where(rows_ref[here] == cols, scores, -1e30)
            largest = jnp.max(scores, axis=1, keepdims=True)
            shifted = jnp.exp(scores - largest).astype(bf16)
            e_ref[hh, here, :] = shifted
            summed = dot(shifted, value)
            inverse = 1.0 / pltpu.roll(summed, HD, axis=1)
            result = (summed * inverse).astype(bf16)
            if hh == 0:
                o_ref[here] = result
                r_ref[here] = inverse
            else:
                o_ref[here] = jnp.where(low, o_ref[here], result)
                r_ref[here] = jnp.where(low, r_ref[here], inverse)


def attend(bias, rows, cols, qkv):
    pairs = D // LANES
    part = lambda at: pl.BlockSpec((LENGTH, LANES), lambda p, at=at: (0, at * pairs + p))
    return pl.pallas_call(
        forward_kernel,
        grid=(pairs,),
        in_specs=[
            pl.BlockSpec((1, 2, REACH), lambda p: (p, 0, 0)),
            pl.BlockSpec((LENGTH, 1), lambda p: (0, 0)),
            pl.BlockSpec((1, LENGTH), lambda p: (0, 0)),
            part(0),
            part(1),
            part(2),
        ],
        out_specs=[
            part(0),
            pl.BlockSpec((2, LENGTH, LENGTH), lambda p: (p, 0, 0)),
            part(0),
        ],
        out_shape=[
            jax.ShapeDtypeStruct((LENGTH, D), bf16),
            jax.ShapeDtypeStruct((H, LENGTH, LENGTH), bf16),
            jax.ShapeDtypeStruct((LENGTH, D), f32),
        ],
        scratch_shapes=[pltpu.VMEM((TILE, 2 * LENGTH - TILE), f32)],
        compiler_params=pltpu.CompilerParams(vmem_limit_bytes=VMEM_LIMIT),
        cost_estimate=pl.CostEstimate(
            flops=16 * H * LENGTH * LENGTH * HD,
            bytes_accessed=40 * 2**20,
            transcendentals=H * LENGTH * LENGTH,
        ),
        name="attend",
    )(bias, rows, cols, qkv, qkv, qkv)


def backward_kernel(
    q_ref, k_ref, v_ref, g_ref, o_ref, r_ref, e_ref, dq_ref, dk_ref, dv_ref, near_ref, t_ref
):
    lane = lax.broadcasted_iota(jnp.int32, (1, LANES), 1)
    low = lane < HD
    blocks = LENGTH // TILE
    block_of = lax.broadcasted_iota(jnp.int32, (LENGTH, LANES), 0) // TILE
    lanes = lax.broadcasted_iota(jnp.int32, (LENGTH, LANES), 1)
    q = q_ref[...]
    k = k_ref[...]
    v = v_ref[...]
    for hh in range(2):
        own = low if hh == 0 else ~low
        free = HD * (1 - hh)
        key = jnp.where(own, k, (lanes - free == block_of).astype(bf16))
        ones = jnp.where((lane == free) | (lane == free + 1), 1.0, 0.0).astype(bf16)
        value = jnp.where(own, v, ones)
        grad = jnp.where(own, g_ref[...].astype(f32) * r_ref[...], 0.0)
        term = -jnp.sum(grad * o_ref[...].astype(f32), axis=1, keepdims=True)
        grad = grad.astype(bf16)
        high = term.astype(bf16)
        rest = (term - high.astype(f32)).astype(bf16)
        joined = jnp.where(lane == free, high, jnp.where(lane == free + 1, rest, grad))
        shifted = e_ref[hh]
        ds = shifted * dot(joined, value, NT).astype(bf16)
        dq = dot(ds, key)
        t_ref[...] = jnp.zeros_like(t_ref)
        leftward = jnp.zeros((1, LANES), f32)
        rightward = jnp.zeros((1, LANES), f32)
        for a in range(blocks):
            first, last = max(a - 1, 0), min(a + 2, blocks)
            at = slice(a * TILE, (a + 1) * TILE)
            to = slice(TILE * (first - a + 1), TILE * (last - a + 1))
            t_ref[:, to] += ds[at, TILE * first : TILE * last].astype(f32)
            totals = jnp.sum(dq[at], axis=0, keepdims=True)
            block = lane - free
            leftward += jnp.where((block >= 0) & (block <= a - 2), totals, 0.0)
            rightward += jnp.where((block >= a + 2) & (block < blocks), totals, 0.0)
        dq = (dq * HD ** (-0.5)).astype(bf16)
        dv = dot(grad, shifted, TN).T.astype(bf16)
        dk = dot(q, ds, TN).T.astype(bf16)
        if hh == 0:
            dq_ref[...] = dq
            dk_ref[...] = dk
            dv_ref[...] = dv
        else:
            dq_ref[...] = jnp.where(low, dq_ref[...], dq)
            dk_ref[...] = jnp.where(low, dk_ref[...], dk)
            dv_ref[...] = jnp.where(low, dv_ref[...], dv)
        diagonals = jnp.concatenate([t_ref[...], jnp.zeros((TILE, TILE), f32)], axis=1)
        row = lax.broadcasted_iota(jnp.int32, (TILE, REACH), 0)
        for bit in range(7):
            moved = pltpu.roll(diagonals, REACH - (1 << bit), axis=1)
            diagonals = jnp.where(((row >> bit) & 1) == 1, moved, diagonals)
        at = lax.broadcasted_iota(jnp.int32, (1, REACH), 1)
        near_ref[0, hh : hh + 1, :] = (
            jnp.sum(diagonals, axis=0, keepdims=True)
            + jnp.where(at == 3 * TILE + 16, jnp.sum(leftward, axis=1, keepdims=True), 0.0)
            + jnp.where(at == 3 * TILE - 1, jnp.sum(rightward, axis=1, keepdims=True), 0.0)
        )


def attend_back(qkv, grad, heads, inverse, shifted, first, pairs):
    every = D // LANES
    part = lambda at: pl.BlockSpec((LENGTH, LANES), lambda p, at=at: (0, at * every + first + p))
    out = pl.BlockSpec((LENGTH, LANES), lambda p: (0, p))
    return pl.pallas_call(
        backward_kernel,
        grid=(pairs,),
        in_specs=[part(0), part(1), part(2), part(0), part(0), part(0)]
        + [pl.BlockSpec((2, LENGTH, LENGTH), lambda p: (first + p, 0, 0))],
        out_specs=[out, out, out]
        + [pl.BlockSpec((1, 2, REACH), lambda p: (p, 0, 0))],
        out_shape=[jax.ShapeDtypeStruct((LENGTH, pairs * LANES), bf16)] * 3
        + [jax.ShapeDtypeStruct((pairs, 2, REACH), f32)],
        scratch_shapes=[pltpu.VMEM((TILE, 3 * TILE), f32)],
        compiler_params=pltpu.CompilerParams(vmem_limit_bytes=VMEM_LIMIT),
        cost_estimate=pl.CostEstimate(
            flops=64 * pairs * LENGTH * LENGTH * HD,
            bytes_accessed=pairs * 6 * 2**20,
            transcendentals=0,
        ),
        name="attend_back",
    )(qkv, qkv, qkv, grad, heads, inverse, shifted)


def params():
    return pltpu.CompilerParams(vmem_limit_bytes=VMEM_LIMIT)


def cost(flops, megabytes):
    return pl.CostEstimate(flops=flops, bytes_accessed=megabytes * 2**20, transcendentals=0)


def put_rows(slot, first, count, rows):
    ids = first + lax.broadcasted_iota(jnp.int32, (count, 1), 0)
    return dot((slot == ids).astype(bf16), rows).astype(bf16)


def slots_kernel(routes_ref, capacity_ref, x_ref, sent_ref, wide_ref, split_ref, *, slots, block):
    step = pl.program_id(0)
    tokens = routes_ref.shape[1]
    experts = capacity_ref.shape[0]

    @pl.when(step == 0)
    def _():
        choice = routes_ref[...]
        chosen = choice == lax.broadcasted_iota(jnp.int32, (experts, 1), 0)
        before = (
            lax.broadcasted_iota(jnp.int32, (tokens, tokens), 0)
            < lax.broadcasted_iota(jnp.int32, (tokens, tokens), 1)
        ).astype(f32)
        counts = dot(chosen.astype(f32).astype(bf16), before.astype(bf16))
        place = jnp.sum(jnp.where(chosen, counts, 0.0), axis=0, keepdims=True).astype(jnp.int32)
        limit = jnp.sum(jnp.where(chosen, capacity_ref[...], 0), axis=0, keepdims=True)
        kept = place < limit
        chunk = slots // 2
        late = (place >= chunk).astype(jnp.int32)
        split = late * experts * chunk + choice * chunk + place - late * chunk
        wide_ref[...] = jnp.where(kept, choice * slots + place, -1)
        split_ref[...] = jnp.where(kept, split, -1)

    sent_ref[...] = put_rows(wide_ref[...], step * block, block, x_ref[...])


def place_rows(routes_row, capacity, rows, slots):
    tokens = rows.shape[0]
    total = capacity.shape[0] * slots
    block = total // 4
    row = pl.BlockSpec((1, tokens), lambda i: (0, 0))
    return pl.pallas_call(
        partial(slots_kernel, slots=slots, block=block),
        grid=(4,),
        in_specs=[
            row,
            pl.BlockSpec(capacity.shape, lambda i: (0, 0)),
            pl.BlockSpec((tokens, D), lambda i: (0, 0)),
        ],
        out_specs=[pl.BlockSpec((block, D), lambda i: (i, 0)), row, row],
        out_shape=[
            jax.ShapeDtypeStruct((total, D), bf16),
            jax.ShapeDtypeStruct((1, tokens), jnp.int32),
            jax.ShapeDtypeStruct((1, tokens), jnp.int32),
        ],
        compiler_params=params(),
        cost_estimate=cost(2 * total * tokens * D, 6),
        name="place_rows",
    )(routes_row, capacity, rows)


def later_kernel(slot_ref, x_ref, sent_ref, *, block, offset):
    first = offset + pl.program_id(0) * block
    sent_ref[...] = put_rows(slot_ref[...], first, block, x_ref[...])


def later_rows(split, rows):
    tokens = rows.shape[0]
    block = tokens // 2
    return pl.pallas_call(
        partial(later_kernel, block=block, offset=tokens),
        grid=(2,),
        in_specs=[
            pl.BlockSpec((1, tokens), lambda i: (0, 0)),
            pl.BlockSpec((tokens, D), lambda i: (0, 0)),
        ],
        out_specs=pl.BlockSpec((block, D), lambda i: (i, 0)),
        out_shape=jax.ShapeDtypeStruct((tokens, D), bf16),
        compiler_params=params(),
        cost_estimate=cost(2 * tokens * tokens * D, 3),
        name="later_rows",
    )(split, rows)


def sides(core, value):
    half = value.shape[1] // 2
    left, right = value[:, :half], value[:, half:]
    return jnp.where(core == 0, left, right), jnp.where(core == 0, right, left)


def joined(core, mine, other):
    return jnp.concatenate(
        [jnp.where(core == 0, mine, other), jnp.where(core == 0, other, mine)], axis=1
    )


def shuffle(order_ref, to_ref):
    source = lax.broadcasted_iota(jnp.int32, (D, 1), 0)
    to_ref[...] = (order_ref[...] == source).astype(bf16)


def project_kernel(
    core_ref, order_ref, gain_ref, x_ref, q0_ref, q1_ref, k0_ref, k1_ref, v0_ref, v1_ref,
    qkv_ref, mixed_ref, shuffle_ref,
):
    core = core_ref[0]

    @pl.when(pl.program_id(0) == 0)
    def _():
        shuffle(order_ref, shuffle_ref)

    x = x_ref[...].astype(f32)
    scale = lax.rsqrt(jnp.mean(x * x, axis=-1, keepdims=True) + epsilon)
    low = (x * scale * gain_ref[...]).astype(bf16)
    mixed_ref[...] = dot(low, shuffle_ref[...]).astype(bf16)
    mine, other = sides(core, low)
    pairs = [(q0_ref, q1_ref), (k0_ref, k1_ref), (v0_ref, v1_ref)]
    for at, (near, far) in enumerate(pairs):
        value = dot(mine, near[...]) + dot(other, far[...])
        value = value * HD ** (-0.5) if at == 0 else value
        qkv_ref[:, at * D : (at + 1) * D] = value.astype(bf16)


ROWS = 256
SMALL = pl.BlockSpec(memory_space=pltpu.SMEM)
VECTOR = pl.BlockSpec((1, D), lambda i: (0, 0))
BLOCK = pl.BlockSpec((ROWS, D), lambda i: (i, 0))
HALF = pl.BlockSpec((D // 2, D), lambda i: (0, 0))


def project(core, order, gain, x, weights):
    tokens = x.shape[0]
    return pl.pallas_call(
        project_kernel,
        grid=(tokens // ROWS,),
        in_specs=[SMALL, VECTOR, VECTOR, BLOCK] + [HALF] * 6,
        out_specs=[pl.BlockSpec((ROWS, 3 * D), lambda i: (i, 0)), BLOCK],
        out_shape=[
            jax.ShapeDtypeStruct((tokens, 3 * D), bf16),
            jax.ShapeDtypeStruct((tokens, D), bf16),
        ],
        scratch_shapes=[pltpu.VMEM((D, D), bf16)],
        compiler_params=params(),
        cost_estimate=cost(8 * tokens * D * D, 12),
        name="project",
    )(core, order, gain, x, *weights)


def hidden_kernel(
    core_ref, order_ref, gain_ref, slot_ref, x_ref, heads_ref, o0_ref, o1_ref,
    hidden_ref, mixed_ref, low_ref, sent_ref, shuffle_ref, *, blocks,
):
    step = pl.program_id(0)
    core = core_ref[0]

    @pl.when(step == 0)
    def _():
        shuffle(order_ref, shuffle_ref)

    @pl.when(step < blocks)
    def _():
        heads = heads_ref[...]
        mixed_ref[...] = dot(heads, shuffle_ref[...]).astype(bf16)
        mine, other = sides(core, heads)
        hidden = x_ref[...].astype(f32) + dot(mine, o0_ref[...]) + dot(other, o1_ref[...])
        scale = lax.rsqrt(jnp.mean(hidden * hidden, axis=-1, keepdims=True) + epsilon)
        hidden_ref[...] = hidden
        at = pl.multiple_of(step * ROWS, ROWS)
        low_ref[pl.ds(at, ROWS), :] = (hidden * scale * gain_ref[...]).astype(bf16)

    @pl.when(step >= blocks)
    def _():
        count = sent_ref.shape[0]
        sent_ref[...] = put_rows(slot_ref[...], (step - blocks) * count, count, low_ref[...])


def make_hidden(core, order, gain, split, x, heads, near, far):
    tokens = x.shape[0]
    blocks = tokens // ROWS
    held = pl.BlockSpec((ROWS, D), lambda i: (jnp.minimum(i, blocks - 1), 0))
    return pl.pallas_call(
        partial(hidden_kernel, blocks=blocks),
        grid=(blocks + 2,),
        in_specs=[SMALL, VECTOR, VECTOR, pl.BlockSpec((1, tokens), lambda i: (0, 0))]
        + [held, held, HALF, HALF],
        out_specs=[
            held,
            held,
            pl.BlockSpec((tokens, D), lambda i: (0, 0)),
            pl.BlockSpec((tokens // 2, D), lambda i: (jnp.maximum(i - blocks, 0), 0)),
        ],
        out_shape=[
            jax.ShapeDtypeStruct((tokens, D), f32),
            jax.ShapeDtypeStruct((tokens, D), bf16),
            jax.ShapeDtypeStruct((tokens, D), bf16),
            jax.ShapeDtypeStruct((tokens, D), bf16),
        ],
        scratch_shapes=[pltpu.VMEM((D, D), bf16)],
        compiler_params=params(),
        cost_estimate=cost(8 * tokens * D * D, 12),
        name="make_hidden",
    )(core, order, gain, split, x, heads, near, far)


def take_rows(slot, total, rows):
    ids = lax.broadcasted_iota(jnp.int32, (1, total), 1)
    return dot((slot == ids).astype(bf16), rows)


def hidden_back_kernel(
    core_ref, gain_ref, slot_ref, back0_ref, back1_ref, cot_ref, hidden_ref, o0_ref, o1_ref,
    grad_ref, branch_ref, heads_ref, term_ref,
):
    core = core_ref[0]
    slot = slot_ref[...]
    total = back0_ref.shape[0]
    hidden = hidden_ref[...]
    grad_ffn = take_rows(slot, total, back0_ref[...]) + take_rows(
        slot - total, total, back1_ref[...]
    )
    scale = lax.rsqrt(jnp.mean(hidden * hidden, axis=-1, keepdims=True) + epsilon)
    weighted = gain_ref[...] * grad_ffn
    along = jnp.mean(weighted * hidden, axis=-1, keepdims=True)
    grad = cot_ref[...].astype(f32) + scale * weighted - hidden * (scale * scale * scale * along)
    branch = grad.astype(bf16)
    grad_ref[...] = grad
    branch_ref[...] = branch
    heads = joined(core, dot(branch, o0_ref[...], NT), dot(branch, o1_ref[...], NT))
    heads_ref[...] = heads.astype(bf16)
    term = jnp.sum(grad_ffn * hidden * scale, axis=0, keepdims=True)

    @pl.when(pl.program_id(0) == 0)
    def _():
        term_ref[...] = jnp.zeros_like(term_ref)

    term_ref[...] += term


def hidden_back(core, gain, slot, back0, back1, cot, hidden, near, far):
    tokens = cot.shape[0]
    every = pl.BlockSpec((tokens, D), lambda i: (0, 0))
    return pl.pallas_call(
        hidden_back_kernel,
        grid=(tokens // ROWS,),
        in_specs=[SMALL, VECTOR, pl.BlockSpec((ROWS, 1), lambda i: (i, 0)), every, every]
        + [BLOCK, BLOCK, HALF, HALF],
        out_specs=[BLOCK, BLOCK, BLOCK, VECTOR],
        out_shape=[
            jax.ShapeDtypeStruct((tokens, D), f32),
            jax.ShapeDtypeStruct((tokens, D), bf16),
            jax.ShapeDtypeStruct((tokens, D), bf16),
            jax.ShapeDtypeStruct((1, D), f32),
        ],
        compiler_params=params(),
        cost_estimate=cost(4 * tokens * tokens * D + 2 * tokens * D * D, 18),
        name="hidden_back",
    )(core, gain, slot, back0, back1, cot, hidden, near, far)


def input_back_kernel(
    core_ref, gain_ref, dq_ref, dk_ref, dv_ref, x_ref, grad_ref,
    q0_ref, q1_ref, k0_ref, k1_ref, v0_ref, v1_ref, out_ref, term_ref,
):
    core = core_ref[0]
    grads = [dq_ref[...], dk_ref[...], dv_ref[...]]
    mine = sum(dot(g, w[...], NT) for g, w in zip(grads, [q0_ref, k0_ref, v0_ref]))
    other = sum(dot(g, w[...], NT) for g, w in zip(grads, [q1_ref, k1_ref, v1_ref]))
    grad_attn = joined(core, mine, other)
    x = x_ref[...].astype(f32)
    scale = lax.rsqrt(jnp.mean(x * x, axis=-1, keepdims=True) + epsilon)
    weighted = gain_ref[...] * grad_attn
    along = jnp.mean(weighted * x, axis=-1, keepdims=True)
    out = grad_ref[...] + scale * weighted - x * (scale * scale * scale * along)
    out_ref[...] = out.astype(bf16)
    term = jnp.sum(grad_attn * x * scale, axis=0, keepdims=True)

    @pl.when(pl.program_id(0) == 0)
    def _():
        term_ref[...] = jnp.zeros_like(term_ref)

    term_ref[...] += term


def input_back(core, gain, grads, x, grad, weights):
    tokens = x.shape[0]
    return pl.pallas_call(
        input_back_kernel,
        grid=(tokens // ROWS,),
        in_specs=[SMALL, VECTOR] + [BLOCK] * 5 + [HALF] * 6,
        out_specs=[BLOCK, VECTOR],
        out_shape=[
            jax.ShapeDtypeStruct((tokens, D), bf16),
            jax.ShapeDtypeStruct((1, D), f32),
        ],
        compiler_params=params(),
        cost_estimate=cost(6 * tokens * D * D, 16),
        name="input_back",
    )(core, gain, *grads, x, grad, *weights)


def output_kernel(slot_ref, rows_ref, hidden_ref, out_ref):
    produced = take_rows(slot_ref[...], rows_ref.shape[0], rows_ref[...])
    out_ref[...] = (hidden_ref[...] + produced).astype(bf16)


def make_output(slot, rows, hidden):
    tokens = hidden.shape[0]
    return pl.pallas_call(
        output_kernel,
        grid=(tokens // ROWS,),
        in_specs=[
            pl.BlockSpec((ROWS, 1), lambda i: (i, 0)),
            pl.BlockSpec(rows.shape, lambda i: (0, 0)),
            BLOCK,
        ],
        out_specs=BLOCK,
        out_shape=jax.ShapeDtypeStruct((tokens, D), bf16),
        compiler_params=params(),
        cost_estimate=cost(2 * rows.shape[0] * tokens * D, 9),
        name="make_output",
    )(slot, rows, hidden)


def expert_kernel(
    me_ref, rows_ref, cot_ref, router_ref, up0_ref, up1_ref, down0_ref, down1_ref,
    sent_ref, back_ref, gp_ref, gl_ref, act_ref, gb_ref,
    out_ref, grow_ref, p_ref, gate_ref, *, experts, steps,
):
    step = pl.program_id(0)
    me = me_ref[0]
    lane = lax.broadcasted_iota(jnp.int32, (1, LANES), 1)

    @pl.when(step == 0)
    def _():
        logits = dot(rows_ref[...], router_ref[...])
        logits = jnp.where(lane < experts, logits, -1e30)
        weight = jnp.exp(logits - jnp.max(logits, axis=1, keepdims=True))
        p = weight / jnp.sum(weight, axis=1, keepdims=True)
        gate = experts * jnp.sum(jnp.where(lane == me, p, 0.0), axis=1, keepdims=True)
        p_ref[...] = p
        gate_ref[...] = gate
        gp_ref[...] = (gate * cot_ref[...].astype(f32)).astype(bf16)
        out_ref[...] = jnp.zeros_like(out_ref)
        grow_ref[...] = jnp.zeros_like(grow_ref)

    mine = step < steps // 2
    up = jnp.where(mine, up0_ref[...], up1_ref[...])
    down = jnp.where(mine, down0_ref[...], down1_ref[...])
    v = dot(rows_ref[...], up)
    scale = np.sqrt(2 / np.pi).astype(np.float32)
    square = v * v
    tanh = jnp.tanh(scale * v * (1.0 + 0.044715 * square))
    half = 0.5 + 0.5 * tanh
    act = (v * half).astype(bf16)
    slope = half + (0.5 * scale) * v * (1.0 - tanh * tanh) * (1.0 + (3 * 0.044715) * square)
    gb = (slope * dot(gp_ref[...], down, NT)).astype(bf16)
    act_ref[0] = act
    gb_ref[0] = gb
    out_ref[...] += dot(act, down)
    grow_ref[...] += dot(gb, up, NT)

    @pl.when(step == steps - 1)
    def _():
        gate = gate_ref[...]
        produced = out_ref[...]
        sent_ref[...] = (gate * produced).astype(bf16)
        grad_gate = jnp.sum(produced * cot_ref[...].astype(f32), axis=1, keepdims=True)
        chosen = jnp.where(lane == me, 1.0, 0.0)
        grad_logits = (grad_gate * gate * (chosen - p_ref[...])).astype(bf16)
        gl_ref[...] = grad_logits
        back_ref[...] = (grow_ref[...] + dot(grad_logits, router_ref[...], NT)).astype(bf16)


def expert_part(me, rows, cot, router, up0, up1, down0, down1, experts):
    count = rows.shape[0]
    half = up0.shape[1]
    tile = 512
    each = half // tile
    steps = 2 * each
    whole = pl.BlockSpec((count, D), lambda f: (0, 0))
    narrow = pl.BlockSpec((count, LANES), lambda f: (0, 0))
    near = lambda f: jnp.minimum(f, each - 1)
    later = lambda f: jnp.maximum(f - each, 0)
    wide = pl.BlockSpec((1, count, tile), lambda f: (f // each, 0, f % each))
    return pl.pallas_call(
        partial(expert_kernel, experts=experts, steps=steps),
        grid=(steps,),
        in_specs=[
            pl.BlockSpec(memory_space=pltpu.SMEM),
            whole,
            whole,
            pl.BlockSpec((D, LANES), lambda f: (0, 0)),
            pl.BlockSpec((D, tile), lambda f: (0, near(f))),
            pl.BlockSpec((D, tile), lambda f: (0, later(f))),
            pl.BlockSpec((tile, D), lambda f: (near(f), 0)),
            pl.BlockSpec((tile, D), lambda f: (later(f), 0)),
        ],
        out_specs=[whole, whole, whole, narrow, wide, wide],
        out_shape=[
            jax.ShapeDtypeStruct((count, D), bf16),
            jax.ShapeDtypeStruct((count, D), bf16),
            jax.ShapeDtypeStruct((count, D), bf16),
            jax.ShapeDtypeStruct((count, LANES), bf16),
            jax.ShapeDtypeStruct((2, count, half), bf16),
            jax.ShapeDtypeStruct((2, count, half), bf16),
        ],
        scratch_shapes=[
            pltpu.VMEM((count, D), f32),
            pltpu.VMEM((count, D), f32),
            pltpu.VMEM((count, LANES), f32),
            pltpu.VMEM((count, 1), f32),
        ],
        compiler_params=pltpu.CompilerParams(vmem_limit_bytes=VMEM_LIMIT),
        cost_estimate=pl.CostEstimate(
            flops=16 * count * D * half,
            bytes_accessed=30 * 2**20,
            transcendentals=2 * count * half,
        ),
        name="expert_part",
    )(me, rows, cot, router, up0, up1, down0, down1)


def up_kernel(*refs):
    rows, gbs = refs[0:2], refs[2:4]
    total = sum(dot(r[...], g[0], TN) for r, g in zip(rows, gbs))
    for received in refs[4:-1]:
        total = total + received[...].astype(f32)
    refs[-1][...] = total.astype(refs[-1].dtype)


def down_kernel(*refs):
    gps, acts = refs[0:2], refs[2:4]
    total = sum(dot(a[0], g[...], TN) for g, a in zip(gps, acts))
    for received in refs[4:-1]:
        total = total + received[...].astype(f32)
    refs[-1][...] = total.astype(refs[-1].dtype)


def weight_sum(kernel, half, narrow, wide, received, name):
    count = narrow[0].shape[0]
    width = wide[0].shape[2]
    tile = 512
    if kernel is up_kernel:
        out = pl.BlockSpec((D, tile), lambda f: (0, f))
        shape = (D, width)
    else:
        out = pl.BlockSpec((tile, D), lambda f: (f, 0))
        shape = (width, D)
    return pl.pallas_call(
        kernel,
        grid=(width // tile,),
        in_specs=[pl.BlockSpec((count, D), lambda f: (0, 0))] * 2
        + [pl.BlockSpec((1, count, tile), lambda f: (half, 0, f))] * 2
        + [out] * len(received),
        out_specs=out,
        out_shape=jax.ShapeDtypeStruct(shape, f32 if received else bf16),
        compiler_params=params(),
        cost_estimate=cost(4 * count * D * width, 16),
        name=name,
    )(*narrow, *wide, *received)


def shards(
    tokens,
    segments,
    routes,
    capacity,
    first_gain,
    query_weight,
    key_weight,
    value_weight,
    output_weight,
    position_bias,
    second_gain,
    router_weight,
    expert_up,
    expert_down,
    cotangent,
):
    owners = lax.axis_size("expert")
    cores = lax.axis_size("dp")
    core = lax.axis_index("dp")
    expert = lax.axis_index("expert")
    token_count = tokens.shape[0]
    experts = capacity.shape[0]
    slots = 2 * token_count // experts
    chunk = slots // 2
    share = D // cores // owners
    bits = owners.bit_length() - 1
    core_at = core.reshape(1).astype(jnp.int32)
    me = expert.reshape(1).astype(jnp.int32)

    def other_core(value):
        return lax.ppermute(value, "dp", [(i, i ^ 1) for i in range(cores)])

    def partner(value, bit):
        return lax.ppermute(value, "expert", [(i, i ^ (1 << bit)) for i in range(owners)])

    def both(mine, other):
        return jnp.where(
            core == 0,
            jnp.concatenate([mine, other], axis=0),
            jnp.concatenate([other, mine], axis=0),
        )

    def exchange(value):
        shape = (experts, -1, D)
        return lax.all_to_all(
            value.reshape(shape), "expert", split_axis=0, concat_axis=0, tiled=True
        )

    cot_sent, wide, split = place_rows(
        routes.reshape(1, token_count), capacity[:, None], cotangent, slots
    )
    cot_arrived = exchange(cot_sent)
    cot_rows = [
        cot_arrived[:, c * chunk : (c + 1) * chunk].reshape(experts * chunk, D) for c in range(2)
    ]
    wide_column = wide.reshape(token_count, 1)
    split_column = split.reshape(token_count, 1)

    small = jnp.concatenate(
        [
            router_weight,
            first_gain[:, None],
            second_gain[:, None],
            jnp.zeros((D // cores, LANES - 2), bf16),
        ],
        axis=1,
    )
    small_full = both(small, other_core(small))
    bias_full = both(position_bias, other_core(position_bias)).astype(f32)
    mixer = []
    for weight in (query_weight, key_weight, value_weight):
        mixer += [weight, other_core(weight)]
    output_far = other_core(output_weight)
    up0 = expert_up[0]
    down0 = expert_down[0]
    up1 = other_core(up0)
    down1 = other_core(down0)
    router = small_full[:, :experts]
    gains = small_full[:, experts : experts + 2].astype(f32).T
    first_full = gains[0:1]
    second_full = gains[1:2]
    router_wide = jnp.pad(router, ((0, 0), (0, LANES - experts)))

    order = np.arange(D).reshape((cores,) + (2,) * bits + (share,))
    order = order.transpose((0,) + tuple(range(bits, 0, -1)) + (bits + 1,)).reshape(cores, -1)
    order = jnp.where(core == 0, order.reshape(1, D), order[::-1].reshape(1, D)).astype(jnp.int32)

    qkv, attn_mixed = project(core_at, order, first_full, tokens, mixer)
    near = np.clip(np.arange(REACH) - REACH // 2, 1 - LENGTH, LENGTH - 1)
    bias = jnp.dot(jnp.asarray(bucket_onehot(near)), bias_full, precision=lax.Precision.HIGHEST)
    bias = bias.T.reshape(H // 2, 2, REACH)
    marks = segments.astype(f32)
    heads_low, shifted, inverse = attend(bias, marks[:, None], marks[None, :], qkv)
    hidden, heads_mixed, ffn_low, sent0 = make_hidden(
        core_at, order, second_full, split, tokens, heads_low, output_weight, output_far
    )

    sent0, *cot_rows = lax.optimization_barrier((sent0, *cot_rows))
    rows0 = exchange(sent0).reshape(token_count, D)
    sent1, rows0 = lax.optimization_barrier((later_rows(split, ffn_low), rows0))
    rows1 = exchange(sent1).reshape(token_count, D)
    arrived = [rows0, rows1]
    parts = [
        expert_part(me, arrived[c], cot_rows[c], router_wide, up0, up1, down0, down1, experts)
        for c in range(2)
    ]
    back0 = exchange(parts[0][1]).reshape(token_count, D)
    back_sent1, back0 = lax.optimization_barrier((parts[1][1], back0))
    back1 = exchange(back_sent1).reshape(token_count, D)

    gps = [part[2] for part in parts]
    acts = [part[4] for part in parts]
    gbs = [part[5] for part in parts]
    weight_sent = [
        weight_sum(up_kernel, 1, arrived, gbs, [], "up_sent"),
        weight_sum(down_kernel, 1, gps, acts, [], "down_sent"),
    ]
    router_term = sum(dot(r, part[3], TN) for r, part in zip(arrived, parts))[:, :experts]
    out_sent = jnp.concatenate(
        [part[0].reshape(experts, chunk, D) for part in parts], axis=1
    )

    out_sent, back0, back1, *weight_sent = lax.optimization_barrier(
        (out_sent, back0, back1, *weight_sent)
    )
    out_rows = exchange(out_sent).reshape(experts * slots, D)
    weight_received = [other_core(value) for value in weight_sent]
    grad_hidden, grad_branch, grad_heads, second_term = hidden_back(
        core_at, second_full, split_column, back0, back1, cotangent, hidden, output_weight, output_far
    )
    dq, dk, dv, near_sums = attend_back(
        qkv, grad_heads, heads_low, inverse, shifted, 0, H // 2
    )
    grads = [dq, dk, dv]

    input_grad, first_term = input_back(core_at, first_full, grads, tokens, grad_hidden, mixer)

    offsets = np.arange(REACH)
    offsets = np.where(offsets < 3 * TILE, offsets - TILE, offsets - TILE - REACH)
    bias_term = jnp.dot(
        jnp.asarray(bucket_onehot(offsets).T),
        near_sums.reshape(H, REACH).T,
        precision=lax.Precision.HIGHEST,
    )
    sizes = [D * experts, D, D, BUCKETS * H]
    totals = jnp.concatenate(
        [part.reshape(-1) for part in (router_term, second_term, first_term, bias_term)]
    ).reshape(-1, LANES)
    totals = totals + other_core(totals)

    terms = [dot(attn_mixed, g, TN) for g in grads] + [dot(heads_mixed, grad_branch, TN)]
    terms = jnp.concatenate([term.astype(bf16) for term in terms], axis=1)
    near_half, far_half = terms[: D // 2], terms[D // 2 :]
    near_half = near_half.astype(f32) + other_core(far_half).astype(f32)
    near_half = near_half.astype(bf16)
    near_half, totals, out_rows = lax.optimization_barrier((near_half, totals, out_rows))
    pieces = jnp.split(near_half, 2, axis=1)
    for step in range(bits):
        if step == 0:
            gbs[0], out_rows = lax.optimization_barrier((gbs[0], out_rows))
            up_grad = weight_sum(up_kernel, 0, arrived, gbs, weight_received[:1], "up_sum")
        if step == 1:
            pieces[0], acts[0] = lax.optimization_barrier((pieces[0], acts[0]))
            down_grad = weight_sum(down_kernel, 0, gps, acts, weight_received[1:], "down_sum")
        if step == 2:
            pieces[0], out_rows = lax.optimization_barrier((pieces[0], out_rows))
            layer_out = make_output(wide_column, out_rows, hidden)
        for at in range(2):
            bit = step ^ 1 if at == 1 and step < 2 else step
            cut = 1 if at == 1 and step == 0 else 0
            piece = pieces[at]
            rows, columns = piece.shape
            piece = piece.reshape(1 << cut, 2, rows >> (cut + 1), columns)
            upper = ((expert >> bit) & 1) == 1
            kept = jnp.where(upper, piece[:, 1], piece[:, 0]).reshape(-1, columns)
            sent = jnp.where(upper, piece[:, 0], piece[:, 1]).reshape(-1, columns)
            kept = kept.astype(f32) + partner(sent, bit).astype(f32)
            pieces[at] = kept if step == bits - 1 else kept.astype(bf16)
        totals = totals + partner(totals, step)
        *pieces, totals = lax.optimization_barrier((*pieces, totals))
    query_grad, key_grad = jnp.split(pieces[0], 2, axis=1)
    value_grad, output_grad = jnp.split(pieces[1], 2, axis=1)

    totals = jnp.split(totals.reshape(-1), np.cumsum(sizes)[:-1])
    first_row = (core * owners + expert) * share
    own = lambda value: lax.dynamic_slice_in_dim(value, first_row, share, axis=0)
    router_grad = own(totals[0].reshape(D, experts))
    second_grad = own(totals[1])
    first_grad = own(totals[2])
    bias_grad = totals[3].reshape(BUCKETS, H)
    return (
        layer_out,
        input_grad,
        first_grad,
        query_grad,
        key_grad,
        value_grad,
        output_grad,
        bias_grad,
        second_grad,
        router_grad,
        up_grad[None],
        down_grad[None],
    )


def solution(mesh):
    both = ("dp", "expert")
    placed = (
        P(both, None),
        P(both),
        P(both, None),
        P(),
        P("dp"),
        P("dp", None),
        P("dp", None),
        P("dp", None),
        P("dp", None),
        P("dp", None),
        P("dp"),
        P("dp", None),
        P("expert", None, "dp"),
        P("expert", "dp", None),
        P(both, None),
    )
    return jax.shard_map(
        shards,
        mesh=mesh,
        in_specs=placed,
        out_specs=(
            P(both, None),
            P(both, None),
            P(both),
            P(both, None),
            P(both, None),
            P(both, None),
            P(both, None),
            P(),
            P(both),
            P(both, None),
            P("expert", None, "dp"),
            P("expert", "dp", None),
        ),
        check_vma=False,
    )
```

```python
from functools import partial

import jax
import jax.numpy as jnp
import numpy as np
from jax import lax
from jax.experimental import pallas as pl
from jax.experimental.pallas import tpu as pltpu
from jax.sharding import PartitionSpec as P

D = 768
H = 12
HD = 64
BUCKETS = 32
MAXDIST = 128
LENGTH = 1024
TILE = 128
REACH = 512
LANES = 128
epsilon = 1e-06
VMEM_LIMIT = 56 * 2**20

bf16 = jnp.bfloat16
f32 = jnp.float32
NN = (((1,), (0,)), ((), ()))
NT = (((1,), (1,)), ((), ()))
TN = (((0,), (0,)), ((), ()))


def dot(left, right, dims=NN):
    return lax.dot_general(left, right, dims, preferred_element_type=f32)


def bucket_table(length, buckets, max_reach):
    offsets = np.arange(-(length - 1), length)
    halved = buckets // 2
    linear = halved // 2
    upward = (offsets > 0).astype(np.int64) * halved
    distance = np.abs(offsets)
    scaled = (
        np.log(np.maximum(distance, 1) / linear) / np.log(max_reach / linear) * (halved - linear)
    )
    logpart = np.minimum(linear + np.floor(np.maximum(scaled, 0.0)).astype(np.int64), halved - 1)
    return (upward + np.where(distance < linear, distance, logpart)).astype(np.int32)


def bucket_onehot(offsets):
    table = bucket_table(LENGTH, BUCKETS, MAXDIST)
    return (table[offsets + LENGTH - 1][:, None] == np.arange(BUCKETS)[None, :]).astype(np.float32)


def forward_kernel(bias_ref, rows_ref, cols_ref, q_ref, k_ref, v_ref, o_ref, e_ref, r_ref, w_ref):
    low = lax.broadcasted_iota(jnp.int32, (1, LANES), 1) < HD
    blocks = LENGTH // TILE
    count = LENGTH // 2
    edge = LENGTH - 2 * TILE
    k = k_ref[...]
    v = v_ref[...]
    cols = cols_ref[...]
    for hh in range(2):
        own = low if hh == 0 else ~low
        near = bias_ref[0, hh : hh + 1, :]
        middle = pltpu.roll(
            jnp.broadcast_to(near, (TILE, REACH)), REACH - TILE, axis=1, stride=1, stride_axis=0
        )
        w_ref[:, :edge] = jnp.broadcast_to(near[:, :1], (TILE, edge))
        w_ref[:, edge : edge + 3 * TILE] = middle[:, : 3 * TILE]
        w_ref[:, edge + 3 * TILE :] = jnp.broadcast_to(near[:, REACH - 1 :], (TILE, edge))
        key = jnp.where(own, k, jnp.zeros_like(k))
        value = jnp.where(own, v, jnp.ones_like(v))
        for base in range(0, LENGTH, count):
            here = slice(base, base + count)
            starts = [TILE * (blocks - 1 - a) for a in range(base // TILE, (base + count) // TILE)]
            bias = jnp.concatenate([w_ref[:, s : s + LENGTH] for s in starts], axis=0)
            scores = dot(q_ref[here], key, NT) + bias
            scores = jnp.where(rows_ref[here] == cols, scores, -1e30)
            largest = jnp.max(scores, axis=1, keepdims=True)
            shifted = jnp.exp(scores - largest).astype(bf16)
            e_ref[hh, here, :] = shifted
            summed = dot(shifted, value)
            inverse = 1.0 / pltpu.roll(summed, HD, axis=1)
            result = (summed * inverse).astype(bf16)
            if hh == 0:
                o_ref[here] = result
                r_ref[here] = inverse
            else:
                o_ref[here] = jnp.where(low, o_ref[here], result)
                r_ref[here] = jnp.where(low, r_ref[here], inverse)


def attend(bias, rows, cols, qkv):
    pairs = D // LANES
    part = lambda at: pl.BlockSpec((LENGTH, LANES), lambda p, at=at: (0, at * pairs + p))
    return pl.pallas_call(
        forward_kernel,
        grid=(pairs,),
        in_specs=[
            pl.BlockSpec((1, 2, REACH), lambda p: (p, 0, 0)),
            pl.BlockSpec((LENGTH, 1), lambda p: (0, 0)),
            pl.BlockSpec((1, LENGTH), lambda p: (0, 0)),
            part(0),
            part(1),
            part(2),
        ],
        out_specs=[
            part(0),
            pl.BlockSpec((2, LENGTH, LENGTH), lambda p: (p, 0, 0)),
            part(0),
        ],
        out_shape=[
            jax.ShapeDtypeStruct((LENGTH, D), bf16),
            jax.ShapeDtypeStruct((H, LENGTH, LENGTH), bf16),
            jax.ShapeDtypeStruct((LENGTH, D), f32),
        ],
        scratch_shapes=[pltpu.VMEM((TILE, 2 * LENGTH - TILE), f32)],
        compiler_params=pltpu.CompilerParams(vmem_limit_bytes=VMEM_LIMIT),
        cost_estimate=pl.CostEstimate(
            flops=16 * H * LENGTH * LENGTH * HD,
            bytes_accessed=40 * 2**20,
            transcendentals=H * LENGTH * LENGTH,
        ),
        name="attend",
    )(bias, rows, cols, qkv, qkv, qkv)


def backward_kernel(
    q_ref, k_ref, v_ref, g_ref, o_ref, r_ref, e_ref, dq_ref, dk_ref, dv_ref, near_ref, t_ref
):
    lane = lax.broadcasted_iota(jnp.int32, (1, LANES), 1)
    low = lane < HD
    blocks = LENGTH // TILE
    block_of = lax.broadcasted_iota(jnp.int32, (LENGTH, LANES), 0) // TILE
    lanes = lax.broadcasted_iota(jnp.int32, (LENGTH, LANES), 1)
    q = q_ref[...]
    k = k_ref[...]
    v = v_ref[...]
    for hh in range(2):
        own = low if hh == 0 else ~low
        free = HD * (1 - hh)
        key = jnp.where(own, k, (lanes - free == block_of).astype(bf16))
        ones = jnp.where((lane == free) | (lane == free + 1), 1.0, 0.0).astype(bf16)
        value = jnp.where(own, v, ones)
        grad = jnp.where(own, g_ref[...].astype(f32) * r_ref[...], 0.0)
        term = -jnp.sum(grad * o_ref[...].astype(f32), axis=1, keepdims=True)
        grad = grad.astype(bf16)
        high = term.astype(bf16)
        rest = (term - high.astype(f32)).astype(bf16)
        joined = jnp.where(lane == free, high, jnp.where(lane == free + 1, rest, grad))
        shifted = e_ref[hh]
        ds = shifted * dot(joined, value, NT).astype(bf16)
        dq = dot(ds, key)
        t_ref[...] = jnp.zeros_like(t_ref)
        leftward = jnp.zeros((1, LANES), f32)
        rightward = jnp.zeros((1, LANES), f32)
        for a in range(blocks):
            first, last = max(a - 1, 0), min(a + 2, blocks)
            at = slice(a * TILE, (a + 1) * TILE)
            to = slice(TILE * (first - a + 1), TILE * (last - a + 1))
            t_ref[:, to] += ds[at, TILE * first : TILE * last].astype(f32)
            totals = jnp.sum(dq[at], axis=0, keepdims=True)
            block = lane - free
            leftward += jnp.where((block >= 0) & (block <= a - 2), totals, 0.0)
            rightward += jnp.where((block >= a + 2) & (block < blocks), totals, 0.0)
        dq = (dq * HD ** (-0.5)).astype(bf16)
        dv = dot(grad, shifted, TN).T.astype(bf16)
        dk = dot(q, ds, TN).T.astype(bf16)
        if hh == 0:
            dq_ref[...] = dq
            dk_ref[...] = dk
            dv_ref[...] = dv
        else:
            dq_ref[...] = jnp.where(low, dq_ref[...], dq)
            dk_ref[...] = jnp.where(low, dk_ref[...], dk)
            dv_ref[...] = jnp.where(low, dv_ref[...], dv)
        diagonals = jnp.concatenate([t_ref[...], jnp.zeros((TILE, TILE), f32)], axis=1)
        row = lax.broadcasted_iota(jnp.int32, (TILE, REACH), 0)
        for bit in range(7):
            moved = pltpu.roll(diagonals, REACH - (1 << bit), axis=1)
            diagonals = jnp.where(((row >> bit) & 1) == 1, moved, diagonals)
        at = lax.broadcasted_iota(jnp.int32, (1, REACH), 1)
        near_ref[0, hh : hh + 1, :] = (
            jnp.sum(diagonals, axis=0, keepdims=True)
            + jnp.where(at == 3 * TILE + 16, jnp.sum(leftward, axis=1, keepdims=True), 0.0)
            + jnp.where(at == 3 * TILE - 1, jnp.sum(rightward, axis=1, keepdims=True), 0.0)
        )


def attend_back(qkv, grad, heads, inverse, shifted, first, pairs):
    every = D // LANES
    part = lambda at: pl.BlockSpec((LENGTH, LANES), lambda p, at=at: (0, at * every + first + p))
    out = pl.BlockSpec((LENGTH, LANES), lambda p: (0, p))
    return pl.pallas_call(
        backward_kernel,
        grid=(pairs,),
        in_specs=[part(0), part(1), part(2), part(0), part(0), part(0)]
        + [pl.BlockSpec((2, LENGTH, LENGTH), lambda p: (first + p, 0, 0))],
        out_specs=[out, out, out]
        + [pl.BlockSpec((1, 2, REACH), lambda p: (p, 0, 0))],
        out_shape=[jax.ShapeDtypeStruct((LENGTH, pairs * LANES), bf16)] * 3
        + [jax.ShapeDtypeStruct((pairs, 2, REACH), f32)],
        scratch_shapes=[pltpu.VMEM((TILE, 3 * TILE), f32)],
        compiler_params=pltpu.CompilerParams(vmem_limit_bytes=VMEM_LIMIT),
        cost_estimate=pl.CostEstimate(
            flops=64 * pairs * LENGTH * LENGTH * HD,
            bytes_accessed=pairs * 6 * 2**20,
            transcendentals=0,
        ),
        name="attend_back",
    )(qkv, qkv, qkv, grad, heads, inverse, shifted)


def params():
    return pltpu.CompilerParams(vmem_limit_bytes=VMEM_LIMIT)


def cost(flops, megabytes):
    return pl.CostEstimate(flops=flops, bytes_accessed=megabytes * 2**20, transcendentals=0)


def put_rows(slot, first, count, rows):
    ids = first + lax.broadcasted_iota(jnp.int32, (count, 1), 0)
    return dot((slot == ids).astype(bf16), rows).astype(bf16)


def slots_kernel(routes_ref, capacity_ref, x_ref, sent_ref, wide_ref, split_ref, *, slots, block):
    step = pl.program_id(0)
    tokens = routes_ref.shape[1]
    experts = capacity_ref.shape[0]

    @pl.when(step == 0)
    def _():
        choice = routes_ref[...]
        chosen = choice == lax.broadcasted_iota(jnp.int32, (experts, 1), 0)
        before = (
            lax.broadcasted_iota(jnp.int32, (tokens, tokens), 0)
            < lax.broadcasted_iota(jnp.int32, (tokens, tokens), 1)
        ).astype(f32)
        counts = dot(chosen.astype(f32).astype(bf16), before.astype(bf16))
        place = jnp.sum(jnp.where(chosen, counts, 0.0), axis=0, keepdims=True).astype(jnp.int32)
        limit = jnp.zeros_like(choice)
        for e in range(experts):
            limit = jnp.where(choice == e, capacity_ref[e], limit)
        kept = place < limit
        chunk = slots // 2
        late = (place >= chunk).astype(jnp.int32)
        split = late * experts * chunk + choice * chunk + place - late * chunk
        wide_ref[...] = jnp.where(kept, choice * slots + place, -1)
        split_ref[...] = jnp.where(kept, split, -1)

    sent_ref[...] = put_rows(wide_ref[...], step * block, block, x_ref[...])


def place_rows(routes_row, capacity, rows, slots):
    tokens = rows.shape[0]
    total = capacity.shape[0] * slots
    block = total // 4
    row = pl.BlockSpec((1, tokens), lambda i: (0, 0))
    return pl.pallas_call(
        partial(slots_kernel, slots=slots, block=block),
        grid=(4,),
        in_specs=[
            row,
            pl.BlockSpec(memory_space=pltpu.SMEM),
            pl.BlockSpec((tokens, D), lambda i: (0, 0)),
        ],
        out_specs=[pl.BlockSpec((block, D), lambda i: (i, 0)), row, row],
        out_shape=[
            jax.ShapeDtypeStruct((total, D), bf16),
            jax.ShapeDtypeStruct((1, tokens), jnp.int32),
            jax.ShapeDtypeStruct((1, tokens), jnp.int32),
        ],
        compiler_params=params(),
        cost_estimate=cost(2 * total * tokens * D, 6),
        name="place_rows",
    )(routes_row, capacity, rows)


def later_kernel(slot_ref, x_ref, sent_ref, *, block, offset):
    first = offset + pl.program_id(0) * block
    sent_ref[...] = put_rows(slot_ref[...], first, block, x_ref[...])


def later_rows(split, rows):
    tokens = rows.shape[0]
    block = tokens // 2
    return pl.pallas_call(
        partial(later_kernel, block=block, offset=tokens),
        grid=(2,),
        in_specs=[
            pl.BlockSpec((1, tokens), lambda i: (0, 0)),
            pl.BlockSpec((tokens, D), lambda i: (0, 0)),
        ],
        out_specs=pl.BlockSpec((block, D), lambda i: (i, 0)),
        out_shape=jax.ShapeDtypeStruct((tokens, D), bf16),
        compiler_params=params(),
        cost_estimate=cost(2 * tokens * tokens * D, 3),
        name="later_rows",
    )(split, rows)


def sides(core, value):
    half = value.shape[1] // 2
    left, right = value[:, :half], value[:, half:]
    return jnp.where(core == 0, left, right), jnp.where(core == 0, right, left)


def joined(core, mine, other):
    return jnp.concatenate(
        [jnp.where(core == 0, mine, other), jnp.where(core == 0, other, mine)], axis=1
    )


def shuffle(order_ref, to_ref):
    source = lax.broadcasted_iota(jnp.int32, (D, 1), 0)
    to_ref[...] = (order_ref[...] == source).astype(bf16)


def project_kernel(
    core_ref, order_ref, gain_ref, x_ref, q0_ref, q1_ref, k0_ref, k1_ref, v0_ref, v1_ref,
    qkv_ref, mixed_ref, shuffle_ref,
):
    core = core_ref[0]

    @pl.when(pl.program_id(0) == 0)
    def _():
        shuffle(order_ref, shuffle_ref)

    x = x_ref[...].astype(f32)
    scale = lax.rsqrt(jnp.mean(x * x, axis=-1, keepdims=True) + epsilon)
    low = (x * scale * gain_ref[...]).astype(bf16)
    mixed_ref[...] = dot(low, shuffle_ref[...]).astype(bf16)
    mine, other = sides(core, low)
    pairs = [(q0_ref, q1_ref), (k0_ref, k1_ref), (v0_ref, v1_ref)]
    for at, (near, far) in enumerate(pairs):
        value = dot(mine, near[...]) + dot(other, far[...])
        value = value * HD ** (-0.5) if at == 0 else value
        qkv_ref[:, at * D : (at + 1) * D] = value.astype(bf16)


ROWS = 256
SMALL = pl.BlockSpec(memory_space=pltpu.SMEM)
VECTOR = pl.BlockSpec((1, D), lambda i: (0, 0))
BLOCK = pl.BlockSpec((ROWS, D), lambda i: (i, 0))
HALF = pl.BlockSpec((D // 2, D), lambda i: (0, 0))


def project(core, order, gain, x, weights):
    tokens = x.shape[0]
    return pl.pallas_call(
        project_kernel,
        grid=(tokens // ROWS,),
        in_specs=[SMALL, VECTOR, VECTOR, BLOCK] + [HALF] * 6,
        out_specs=[pl.BlockSpec((ROWS, 3 * D), lambda i: (i, 0)), BLOCK],
        out_shape=[
            jax.ShapeDtypeStruct((tokens, 3 * D), bf16),
            jax.ShapeDtypeStruct((tokens, D), bf16),
        ],
        scratch_shapes=[pltpu.VMEM((D, D), bf16)],
        compiler_params=params(),
        cost_estimate=cost(8 * tokens * D * D, 12),
        name="project",
    )(core, order, gain, x, *weights)


def hidden_kernel(
    core_ref, order_ref, gain_ref, slot_ref, x_ref, heads_ref, o0_ref, o1_ref,
    hidden_ref, mixed_ref, low_ref, sent_ref, shuffle_ref, *, blocks,
):
    step = pl.program_id(0)
    core = core_ref[0]

    @pl.when(step == 0)
    def _():
        shuffle(order_ref, shuffle_ref)

    @pl.when(step < blocks)
    def _():
        heads = heads_ref[...]
        mixed_ref[...] = dot(heads, shuffle_ref[...]).astype(bf16)
        mine, other = sides(core, heads)
        hidden = x_ref[...].astype(f32) + dot(mine, o0_ref[...]) + dot(other, o1_ref[...])
        scale = lax.rsqrt(jnp.mean(hidden * hidden, axis=-1, keepdims=True) + epsilon)
        hidden_ref[...] = hidden
        at = pl.multiple_of(step * ROWS, ROWS)
        low_ref[pl.ds(at, ROWS), :] = (hidden * scale * gain_ref[...]).astype(bf16)

    @pl.when(step >= blocks)
    def _():
        count = sent_ref.shape[0]
        sent_ref[...] = put_rows(slot_ref[...], (step - blocks) * count, count, low_ref[...])


def make_hidden(core, order, gain, split, x, heads, near, far):
    tokens = x.shape[0]
    blocks = tokens // ROWS
    held = pl.BlockSpec((ROWS, D), lambda i: (jnp.minimum(i, blocks - 1), 0))
    return pl.pallas_call(
        partial(hidden_kernel, blocks=blocks),
        grid=(blocks + 2,),
        in_specs=[SMALL, VECTOR, VECTOR, pl.BlockSpec((1, tokens), lambda i: (0, 0))]
        + [held, held, HALF, HALF],
        out_specs=[
            held,
            held,
            pl.BlockSpec((tokens, D), lambda i: (0, 0)),
            pl.BlockSpec((tokens // 2, D), lambda i: (jnp.maximum(i - blocks, 0), 0)),
        ],
        out_shape=[
            jax.ShapeDtypeStruct((tokens, D), f32),
            jax.ShapeDtypeStruct((tokens, D), bf16),
            jax.ShapeDtypeStruct((tokens, D), bf16),
            jax.ShapeDtypeStruct((tokens, D), bf16),
        ],
        scratch_shapes=[pltpu.VMEM((D, D), bf16)],
        compiler_params=params(),
        cost_estimate=cost(8 * tokens * D * D, 12),
        name="make_hidden",
    )(core, order, gain, split, x, heads, near, far)


def take_rows(slot, total, rows):
    ids = lax.broadcasted_iota(jnp.int32, (1, total), 1)
    return dot((slot == ids).astype(bf16), rows)


def hidden_back_kernel(
    core_ref, gain_ref, slot_ref, back0_ref, back1_ref, cot_ref, hidden_ref, o0_ref, o1_ref,
    grad_ref, branch_ref, heads_ref, term_ref,
):
    core = core_ref[0]
    slot = slot_ref[...]
    total = back0_ref.shape[0]
    hidden = hidden_ref[...]
    grad_ffn = take_rows(slot, total, back0_ref[...]) + take_rows(
        slot - total, total, back1_ref[...]
    )
    scale = lax.rsqrt(jnp.mean(hidden * hidden, axis=-1, keepdims=True) + epsilon)
    weighted = gain_ref[...] * grad_ffn
    along = jnp.mean(weighted * hidden, axis=-1, keepdims=True)
    grad = cot_ref[...].astype(f32) + scale * weighted - hidden * (scale * scale * scale * along)
    branch = grad.astype(bf16)
    grad_ref[...] = grad
    branch_ref[...] = branch
    heads = joined(core, dot(branch, o0_ref[...], NT), dot(branch, o1_ref[...], NT))
    heads_ref[...] = heads.astype(bf16)
    term = jnp.sum(grad_ffn * hidden * scale, axis=0, keepdims=True)

    @pl.when(pl.program_id(0) == 0)
    def _():
        term_ref[...] = jnp.zeros_like(term_ref)

    term_ref[...] += term


def hidden_back(core, gain, slot, back0, back1, cot, hidden, near, far):
    tokens = cot.shape[0]
    every = pl.BlockSpec((tokens, D), lambda i: (0, 0))
    return pl.pallas_call(
        hidden_back_kernel,
        grid=(tokens // ROWS,),
        in_specs=[SMALL, VECTOR, pl.BlockSpec((ROWS, 1), lambda i: (i, 0)), every, every]
        + [BLOCK, BLOCK, HALF, HALF],
        out_specs=[BLOCK, BLOCK, BLOCK, VECTOR],
        out_shape=[
            jax.ShapeDtypeStruct((tokens, D), f32),
            jax.ShapeDtypeStruct((tokens, D), bf16),
            jax.ShapeDtypeStruct((tokens, D), bf16),
            jax.ShapeDtypeStruct((1, D), f32),
        ],
        compiler_params=params(),
        cost_estimate=cost(4 * tokens * tokens * D + 2 * tokens * D * D, 18),
        name="hidden_back",
    )(core, gain, slot, back0, back1, cot, hidden, near, far)


def input_back_kernel(
    core_ref, gain_ref, dq_ref, dk_ref, dv_ref, x_ref, grad_ref,
    q0_ref, q1_ref, k0_ref, k1_ref, v0_ref, v1_ref, out_ref, term_ref,
):
    core = core_ref[0]
    grads = [dq_ref[...], dk_ref[...], dv_ref[...]]
    mine = sum(dot(g, w[...], NT) for g, w in zip(grads, [q0_ref, k0_ref, v0_ref]))
    other = sum(dot(g, w[...], NT) for g, w in zip(grads, [q1_ref, k1_ref, v1_ref]))
    grad_attn = joined(core, mine, other)
    x = x_ref[...].astype(f32)
    scale = lax.rsqrt(jnp.mean(x * x, axis=-1, keepdims=True) + epsilon)
    weighted = gain_ref[...] * grad_attn
    along = jnp.mean(weighted * x, axis=-1, keepdims=True)
    out = grad_ref[...] + scale * weighted - x * (scale * scale * scale * along)
    out_ref[...] = out.astype(bf16)
    term = jnp.sum(grad_attn * x * scale, axis=0, keepdims=True)

    @pl.when(pl.program_id(0) == 0)
    def _():
        term_ref[...] = jnp.zeros_like(term_ref)

    term_ref[...] += term


def input_back(core, gain, grads, x, grad, weights):
    tokens = x.shape[0]
    return pl.pallas_call(
        input_back_kernel,
        grid=(tokens // ROWS,),
        in_specs=[SMALL, VECTOR] + [BLOCK] * 5 + [HALF] * 6,
        out_specs=[BLOCK, VECTOR],
        out_shape=[
            jax.ShapeDtypeStruct((tokens, D), bf16),
            jax.ShapeDtypeStruct((1, D), f32),
        ],
        compiler_params=params(),
        cost_estimate=cost(6 * tokens * D * D, 16),
        name="input_back",
    )(core, gain, *grads, x, grad, *weights)


def output_kernel(slot_ref, rows_ref, hidden_ref, out_ref):
    produced = take_rows(slot_ref[...], rows_ref.shape[0], rows_ref[...])
    out_ref[...] = (hidden_ref[...] + produced).astype(bf16)


def make_output(slot, rows, hidden):
    tokens = hidden.shape[0]
    return pl.pallas_call(
        output_kernel,
        grid=(tokens // ROWS,),
        in_specs=[
            pl.BlockSpec((ROWS, 1), lambda i: (i, 0)),
            pl.BlockSpec(rows.shape, lambda i: (0, 0)),
            BLOCK,
        ],
        out_specs=BLOCK,
        out_shape=jax.ShapeDtypeStruct((tokens, D), bf16),
        compiler_params=params(),
        cost_estimate=cost(2 * rows.shape[0] * tokens * D, 9),
        name="make_output",
    )(slot, rows, hidden)


def expert_kernel(
    me_ref, rows_ref, cot_ref, router_ref, up0_ref, up1_ref, down0_ref, down1_ref,
    sent_ref, back_ref, gp_ref, gl_ref, act_ref, gb_ref,
    out_ref, grow_ref, p_ref, gate_ref, *, experts, steps,
):
    step = pl.program_id(0)
    me = me_ref[0]
    lane = lax.broadcasted_iota(jnp.int32, (1, LANES), 1)

    @pl.when(step == 0)
    def _():
        logits = dot(rows_ref[...], router_ref[...])
        logits = jnp.where(lane < experts, logits, -1e30)
        weight = jnp.exp(logits - jnp.max(logits, axis=1, keepdims=True))
        p = weight / jnp.sum(weight, axis=1, keepdims=True)
        gate = experts * jnp.sum(jnp.where(lane == me, p, 0.0), axis=1, keepdims=True)
        p_ref[...] = p
        gate_ref[...] = gate
        gp_ref[...] = (gate * cot_ref[...].astype(f32)).astype(bf16)
        out_ref[...] = jnp.zeros_like(out_ref)
        grow_ref[...] = jnp.zeros_like(grow_ref)

    mine = step < steps // 2
    up = jnp.where(mine, up0_ref[...], up1_ref[...])
    down = jnp.where(mine, down0_ref[...], down1_ref[...])
    v = dot(rows_ref[...], up)
    scale = np.sqrt(2 / np.pi).astype(np.float32)
    square = v * v
    tanh = jnp.tanh(scale * v * (1.0 + 0.044715 * square))
    half = 0.5 + 0.5 * tanh
    act = (v * half).astype(bf16)
    slope = half + (0.5 * scale) * v * (1.0 - tanh * tanh) * (1.0 + (3 * 0.044715) * square)
    gb = (slope * dot(gp_ref[...], down, NT)).astype(bf16)
    act_ref[0] = act
    gb_ref[0] = gb
    out_ref[...] += dot(act, down)
    grow_ref[...] += dot(gb, up, NT)

    @pl.when(step == steps - 1)
    def _():
        gate = gate_ref[...]
        produced = out_ref[...]
        sent_ref[...] = (gate * produced).astype(bf16)
        grad_gate = jnp.sum(produced * cot_ref[...].astype(f32), axis=1, keepdims=True)
        chosen = jnp.where(lane == me, 1.0, 0.0)
        grad_logits = (grad_gate * gate * (chosen - p_ref[...])).astype(bf16)
        gl_ref[...] = grad_logits
        back_ref[...] = (grow_ref[...] + dot(grad_logits, router_ref[...], NT)).astype(bf16)


def expert_part(me, rows, cot, router, up0, up1, down0, down1, experts):
    count = rows.shape[0]
    half = up0.shape[1]
    tile = 512
    each = half // tile
    steps = 2 * each
    whole = pl.BlockSpec((count, D), lambda f: (0, 0))
    narrow = pl.BlockSpec((count, LANES), lambda f: (0, 0))
    near = lambda f: jnp.minimum(f, each - 1)
    later = lambda f: jnp.maximum(f - each, 0)
    wide = pl.BlockSpec((1, count, tile), lambda f: (f // each, 0, f % each))
    return pl.pallas_call(
        partial(expert_kernel, experts=experts, steps=steps),
        grid=(steps,),
        in_specs=[
            pl.BlockSpec(memory_space=pltpu.SMEM),
            whole,
            whole,
            pl.BlockSpec((D, LANES), lambda f: (0, 0)),
            pl.BlockSpec((D, tile), lambda f: (0, near(f))),
            pl.BlockSpec((D, tile), lambda f: (0, later(f))),
            pl.BlockSpec((tile, D), lambda f: (near(f), 0)),
            pl.BlockSpec((tile, D), lambda f: (later(f), 0)),
        ],
        out_specs=[whole, whole, whole, narrow, wide, wide],
        out_shape=[
            jax.ShapeDtypeStruct((count, D), bf16),
            jax.ShapeDtypeStruct((count, D), bf16),
            jax.ShapeDtypeStruct((count, D), bf16),
            jax.ShapeDtypeStruct((count, LANES), bf16),
            jax.ShapeDtypeStruct((2, count, half), bf16),
            jax.ShapeDtypeStruct((2, count, half), bf16),
        ],
        scratch_shapes=[
            pltpu.VMEM((count, D), f32),
            pltpu.VMEM((count, D), f32),
            pltpu.VMEM((count, LANES), f32),
            pltpu.VMEM((count, 1), f32),
        ],
        compiler_params=pltpu.CompilerParams(vmem_limit_bytes=44 * 2**20),
        cost_estimate=pl.CostEstimate(
            flops=16 * count * D * half,
            bytes_accessed=30 * 2**20,
            transcendentals=2 * count * half,
        ),
        name="expert_part",
    )(me, rows, cot, router, up0, up1, down0, down1)


def terms_kernel(attn_ref, heads_ref, *refs):
    near_refs, far_refs = refs[4:6], refs[6:8]
    step = pl.program_id(0)
    half = D // 2
    for at in range(4):

        @pl.when(step == at)
        def _(at=at):
            left = attn_ref if at < 3 else heads_ref
            total = dot(left[...], refs[at][...], TN).astype(bf16)
            near_refs[at // 2][...] = total[:half]
            far_refs[at // 2][...] = total[half:]


def weight_terms(attn, heads, grads):
    tokens = attn.shape[0]
    whole = pl.BlockSpec((tokens, D), lambda i: (0, 0))
    early = pl.BlockSpec((D // 2, D), lambda i: (0, jnp.minimum(i, 1)))
    late = pl.BlockSpec((D // 2, D), lambda i: (0, jnp.maximum(i - 2, 0)))
    return pl.pallas_call(
        terms_kernel,
        grid=(4,),
        in_specs=[whole] * 6,
        out_specs=[early, late, early, late],
        out_shape=[jax.ShapeDtypeStruct((D // 2, 2 * D), bf16)] * 4,
        compiler_params=params(),
        cost_estimate=cost(8 * tokens * D * D, 14),
        name="weight_terms",
    )(attn, heads, *grads)


def up_kernel(*refs):
    rows, gbs = refs[0:2], refs[2:4]
    total = sum(dot(r[...], g[0], TN) for r, g in zip(rows, gbs))
    for received in refs[4:-1]:
        total = total + received[...].astype(f32)
    refs[-1][...] = total.astype(refs[-1].dtype)


def down_kernel(*refs):
    gps, acts = refs[0:2], refs[2:4]
    total = sum(dot(a[0], g[...], TN) for g, a in zip(gps, acts))
    for received in refs[4:-1]:
        total = total + received[...].astype(f32)
    refs[-1][...] = total.astype(refs[-1].dtype)


def weight_sum(kernel, half, narrow, wide, received, name, kind=f32):
    count = narrow[0].shape[0]
    width = wide[0].shape[2]
    tile = 512
    if kernel is up_kernel:
        out = pl.BlockSpec((D, tile), lambda f: (0, f))
        shape = (D, width)
    else:
        out = pl.BlockSpec((tile, D), lambda f: (f, 0))
        shape = (width, D)
    return pl.pallas_call(
        kernel,
        grid=(width // tile,),
        in_specs=[pl.BlockSpec((count, D), lambda f: (0, 0))] * 2
        + [pl.BlockSpec((1, count, tile), lambda f: (half, 0, f))] * 2
        + [out] * len(received),
        out_specs=out,
        out_shape=jax.ShapeDtypeStruct(shape, kind),
        compiler_params=params(),
        cost_estimate=cost(4 * count * D * width, 16),
        name=name,
    )(*narrow, *wide, *received)


def shards(
    tokens,
    segments,
    routes,
    capacity,
    first_gain,
    query_weight,
    key_weight,
    value_weight,
    output_weight,
    position_bias,
    second_gain,
    router_weight,
    expert_up,
    expert_down,
    cotangent,
):
    owners = lax.axis_size("expert")
    cores = lax.axis_size("dp")
    core = lax.axis_index("dp")
    expert = lax.axis_index("expert")
    token_count = tokens.shape[0]
    experts = capacity.shape[0]
    slots = 2 * token_count // experts
    chunk = slots // 2
    share = D // cores // owners
    bits = owners.bit_length() - 1
    core_at = core.reshape(1).astype(jnp.int32)
    me = expert.reshape(1).astype(jnp.int32)

    def other_core(value):
        return lax.ppermute(value, "dp", [(i, i ^ 1) for i in range(cores)])

    def partner(value, bit):
        return lax.ppermute(value, "expert", [(i, i ^ (1 << bit)) for i in range(owners)])

    def across(value):
        mask = 3 << (bits - 2)
        return lax.ppermute(value, "expert", [(i, i ^ mask) for i in range(owners)])

    def both(mine, other):
        return jnp.where(
            core == 0,
            jnp.concatenate([mine, other], axis=0),
            jnp.concatenate([other, mine], axis=0),
        )

    def exchange(value):
        shape = (experts, -1, D)
        return lax.all_to_all(
            value.reshape(shape), "expert", split_axis=0, concat_axis=0, tiled=True
        )

    cot_sent, wide, split = place_rows(
        routes.reshape(1, token_count), capacity, cotangent, slots
    )
    cot_arrived = exchange(cot_sent)
    cot_rows = [
        cot_arrived[:, c * chunk : (c + 1) * chunk].reshape(experts * chunk, D) for c in range(2)
    ]
    wide_column = wide.reshape(token_count, 1)
    split_column = split.reshape(token_count, 1)

    small = jnp.concatenate(
        [
            router_weight,
            first_gain[:, None],
            second_gain[:, None],
            jnp.zeros((D // cores, LANES - 2), bf16),
        ],
        axis=1,
    )
    small_full = both(small, other_core(small))
    bias_full = both(position_bias, other_core(position_bias)).astype(f32)
    mixer = []
    for weight in (query_weight, key_weight, value_weight):
        mixer += [weight, other_core(weight)]
    output_far = other_core(output_weight)
    up0 = expert_up[0]
    down0 = expert_down[0]
    up1 = other_core(up0)
    down1 = other_core(down0)
    router = small_full[:, :experts]
    gains = small_full[:, experts : experts + 2].astype(f32).T
    first_full = gains[0:1]
    second_full = gains[1:2]
    router_wide = jnp.pad(router, ((0, 0), (0, LANES - experts)))

    order = np.arange(D).reshape((cores,) + (2,) * bits + (share,))
    order = order.transpose((0,) + tuple(range(bits, 0, -1)) + (bits + 1,)).reshape(cores, -1)
    order = jnp.where(core == 0, order.reshape(1, D), order[::-1].reshape(1, D)).astype(jnp.int32)

    qkv, attn_mixed = project(core_at, order, first_full, tokens, mixer)
    near = np.clip(np.arange(REACH) - REACH // 2, 1 - LENGTH, LENGTH - 1)
    bias = jnp.dot(jnp.asarray(bucket_onehot(near)), bias_full, precision=lax.Precision.HIGHEST)
    bias = bias.T.reshape(H // 2, 2, REACH)
    marks = segments.astype(f32)
    heads_low, shifted, inverse = attend(bias, marks[:, None], marks[None, :], qkv)
    hidden, heads_mixed, ffn_low, sent0 = make_hidden(
        core_at, order, second_full, split, tokens, heads_low, output_weight, output_far
    )

    sent0, *cot_rows = lax.optimization_barrier((sent0, *cot_rows))
    rows0 = exchange(sent0).reshape(token_count, D)
    sent1, rows0 = lax.optimization_barrier((later_rows(split, ffn_low), rows0))
    rows1 = exchange(sent1).reshape(token_count, D)
    arrived = [rows0, rows1]
    parts = [
        expert_part(me, arrived[c], cot_rows[c], router_wide, up0, up1, down0, down1, experts)
        for c in range(2)
    ]
    back0 = exchange(parts[0][1]).reshape(token_count, D)
    back_sent1, back0 = lax.optimization_barrier((parts[1][1], back0))
    back1 = exchange(back_sent1).reshape(token_count, D)

    gps = [part[2] for part in parts]
    acts = [part[4] for part in parts]
    gbs = [part[5] for part in parts]
    weight_sent = [
        weight_sum(up_kernel, 1, arrived, gbs, [], "up_sent", bf16),
        weight_sum(down_kernel, 1, gps, acts, [], "down_sent", bf16),
        weight_sum(up_kernel, 0, arrived, gbs, [], "up_own"),
    ]
    router_term = sum(dot(r, part[3], TN) for r, part in zip(arrived, parts))[:, :experts]
    out_sent = jnp.concatenate(
        [part[0].reshape(experts, chunk, D) for part in parts], axis=1
    )

    out_sent, back0, back1, *weight_sent = lax.optimization_barrier(
        (out_sent, back0, back1, *weight_sent)
    )
    out_rows = exchange(out_sent).reshape(experts * slots, D)
    weight_received = [other_core(value) for value in weight_sent[:2]]
    grad_hidden, grad_branch, grad_heads, second_term = hidden_back(
        core_at, second_full, split_column, back0, back1, cotangent, hidden, output_weight, output_far
    )
    dq, dk, dv, near_sums = attend_back(
        qkv, grad_heads, heads_low, inverse, shifted, 0, H // 2
    )
    grads = [dq, dk, dv]

    input_grad, first_term = input_back(core_at, first_full, grads, tokens, grad_hidden, mixer)

    offsets = np.arange(REACH)
    offsets = np.where(offsets < 3 * TILE, offsets - TILE, offsets - TILE - REACH)
    bias_term = jnp.dot(
        jnp.asarray(bucket_onehot(offsets).T),
        near_sums.reshape(H, REACH).T,
        precision=lax.Precision.HIGHEST,
    )
    sizes = [D * experts, D, D, BUCKETS * H]
    totals = jnp.concatenate(
        [part.reshape(-1) for part in (router_term, second_term, first_term, bias_term)]
    ).reshape(-1, LANES)
    *pieces, far0, far1 = weight_terms(attn_mixed, heads_mixed, [*grads, grad_branch])
    received = [other_core(far0), other_core(far1)]
    *received, totals, out_rows = lax.optimization_barrier((*received, totals, out_rows))
    pieces = [
        (near.astype(f32) + far.astype(f32)).astype(bf16) for near, far in zip(pieces, received)
    ]
    for step in range(bits):
        if step == 0:
            acts[0], out_rows = lax.optimization_barrier((acts[0], out_rows))
            down_grad = weight_sum(down_kernel, 0, gps, acts, weight_received[1:], "down_sum")
        if step == 1:
            pieces[0], out_rows = lax.optimization_barrier((pieces[0], out_rows))
            layer_out = make_output(wide_column, out_rows, hidden)
        if step == 2:
            pieces[0], up_own = lax.optimization_barrier((pieces[0], weight_sent[2]))
            up_grad = up_own + weight_received[0].astype(f32)
        if step == 2:
            pieces = [jnp.concatenate(pieces, axis=1)]
        for at in range(len(pieces)):
            bit = step ^ 1 if at == 1 else step
            cut = 1 if at == 1 and step == 0 else 0
            piece = pieces[at]
            rows, columns = piece.shape
            piece = piece.reshape(1 << cut, 2, rows >> (cut + 1), columns)
            upper = ((expert >> bit) & 1) == 1
            kept = jnp.where(upper, piece[:, 1], piece[:, 0]).reshape(-1, columns)
            sent = jnp.where(upper, piece[:, 0], piece[:, 1]).reshape(-1, columns)
            kept = kept.astype(f32) + partner(sent, bit).astype(f32)
            pieces[at] = kept if step == bits - 1 else kept.astype(bf16)
        if step == 0:
            totals = totals + other_core(totals)
        elif step < bits - 1:
            totals = totals + partner(totals, step - 1)
        else:
            far = [partner(totals, bits - 2), partner(totals, bits - 1)]
            totals = totals + far[0] + (far[1] + across(totals))
        *pieces, totals = lax.optimization_barrier((*pieces, totals))
    query_grad, key_grad, value_grad, output_grad = jnp.split(pieces[0], 4, axis=1)

    totals = jnp.split(totals.reshape(-1), np.cumsum(sizes)[:-1])
    first_row = (core * owners + expert) * share
    own = lambda value: lax.dynamic_slice_in_dim(value, first_row, share, axis=0)
    router_grad = own(totals[0].reshape(D, experts))
    second_grad = own(totals[1])
    first_grad = own(totals[2])
    bias_grad = totals[3].reshape(BUCKETS, H)
    return (
        layer_out,
        input_grad,
        first_grad,
        query_grad,
        key_grad,
        value_grad,
        output_grad,
        bias_grad,
        second_grad,
        router_grad,
        up_grad[None],
        down_grad[None],
    )


def solution(mesh):
    both = ("dp", "expert")
    placed = (
        P(both, None),
        P(both),
        P(both, None),
        P(),
        P("dp"),
        P("dp", None),
        P("dp", None),
        P("dp", None),
        P("dp", None),
        P("dp", None),
        P("dp"),
        P("dp", None),
        P("expert", None, "dp"),
        P("expert", "dp", None),
        P(both, None),
    )
    return jax.shard_map(
        shards,
        mesh=mesh,
        in_specs=placed,
        out_specs=(
            P(both, None),
            P(both, None),
            P(both),
            P(both, None),
            P(both, None),
            P(both, None),
            P(both, None),
            P(),
            P(both),
            P(both, None),
            P("expert", None, "dp"),
            P("expert", "dp", None),
        ),
        check_vma=False,
    )
```

```python
from functools import partial

import jax
import jax.numpy as jnp
import numpy as np
from jax import lax
from jax.experimental import pallas as pl
from jax.experimental.pallas import tpu as pltpu
from jax.sharding import PartitionSpec as P

D = 768
H = 12
HD = 64
BUCKETS = 32
MAXDIST = 128
LENGTH = 1024
TILE = 128
REACH = 512
LANES = 128
epsilon = 1e-06
VMEM_LIMIT = 56 * 2**20

bf16 = jnp.bfloat16
f32 = jnp.float32
NN = (((1,), (0,)), ((), ()))
NT = (((1,), (1,)), ((), ()))
TN = (((0,), (0,)), ((), ()))


def dot(left, right, dims=NN):
    return lax.dot_general(left, right, dims, preferred_element_type=f32)


def bucket_table(length, buckets, max_reach):
    offsets = np.arange(-(length - 1), length)
    halved = buckets // 2
    linear = halved // 2
    upward = (offsets > 0).astype(np.int64) * halved
    distance = np.abs(offsets)
    scaled = (
        np.log(np.maximum(distance, 1) / linear) / np.log(max_reach / linear) * (halved - linear)
    )
    logpart = np.minimum(linear + np.floor(np.maximum(scaled, 0.0)).astype(np.int64), halved - 1)
    return (upward + np.where(distance < linear, distance, logpart)).astype(np.int32)


def bucket_onehot(offsets):
    table = bucket_table(LENGTH, BUCKETS, MAXDIST)
    return (table[offsets + LENGTH - 1][:, None] == np.arange(BUCKETS)[None, :]).astype(np.float32)


def forward_kernel(bias_ref, rows_ref, cols_ref, q_ref, k_ref, v_ref, o_ref, e_ref, r_ref, w_ref):
    low = lax.broadcasted_iota(jnp.int32, (1, LANES), 1) < HD
    blocks = LENGTH // TILE
    count = LENGTH // 2
    edge = LENGTH - 2 * TILE
    k = k_ref[...]
    v = v_ref[...]
    cols = cols_ref[...]
    for hh in range(2):
        own = low if hh == 0 else ~low
        near = bias_ref[0, hh : hh + 1, :]
        middle = pltpu.roll(
            jnp.broadcast_to(near, (TILE, REACH)), REACH - TILE, axis=1, stride=1, stride_axis=0
        )
        w_ref[:, :edge] = jnp.broadcast_to(near[:, :1], (TILE, edge))
        w_ref[:, edge : edge + 3 * TILE] = middle[:, : 3 * TILE]
        w_ref[:, edge + 3 * TILE :] = jnp.broadcast_to(near[:, REACH - 1 :], (TILE, edge))
        key = jnp.where(own, k, jnp.zeros_like(k))
        value = jnp.where(own, v, jnp.ones_like(v))
        for base in range(0, LENGTH, count):
            here = slice(base, base + count)
            starts = [TILE * (blocks - 1 - a) for a in range(base // TILE, (base + count) // TILE)]
            bias = jnp.concatenate([w_ref[:, s : s + LENGTH] for s in starts], axis=0)
            scores = dot(q_ref[here], key, NT) + bias
            scores = jnp.where(rows_ref[here] == cols, scores, -1e30)
            largest = jnp.max(scores, axis=1, keepdims=True)
            shifted = jnp.exp(scores - largest).astype(bf16)
            e_ref[hh, here, :] = shifted
            summed = dot(shifted, value)
            inverse = 1.0 / pltpu.roll(summed, HD, axis=1)
            result = (summed * inverse).astype(bf16)
            if hh == 0:
                o_ref[here] = result
                r_ref[here] = inverse
            else:
                o_ref[here] = jnp.where(low, o_ref[here], result)
                r_ref[here] = jnp.where(low, r_ref[here], inverse)


def attend(bias, rows, cols, qkv):
    pairs = D // LANES
    part = lambda at: pl.BlockSpec((LENGTH, LANES), lambda p, at=at: (0, at * pairs + p))
    return pl.pallas_call(
        forward_kernel,
        grid=(pairs,),
        in_specs=[
            pl.BlockSpec((1, 2, REACH), lambda p: (p, 0, 0)),
            pl.BlockSpec((LENGTH, 1), lambda p: (0, 0)),
            pl.BlockSpec((1, LENGTH), lambda p: (0, 0)),
            part(0),
            part(1),
            part(2),
        ],
        out_specs=[
            part(0),
            pl.BlockSpec((2, LENGTH, LENGTH), lambda p: (p, 0, 0)),
            part(0),
        ],
        out_shape=[
            jax.ShapeDtypeStruct((LENGTH, D), bf16),
            jax.ShapeDtypeStruct((H, LENGTH, LENGTH), bf16),
            jax.ShapeDtypeStruct((LENGTH, D), f32),
        ],
        scratch_shapes=[pltpu.VMEM((TILE, 2 * LENGTH - TILE), f32)],
        compiler_params=pltpu.CompilerParams(vmem_limit_bytes=VMEM_LIMIT),
        cost_estimate=pl.CostEstimate(
            flops=16 * H * LENGTH * LENGTH * HD,
            bytes_accessed=40 * 2**20,
            transcendentals=H * LENGTH * LENGTH,
        ),
        name="attend",
    )(bias, rows, cols, qkv, qkv, qkv)


def backward_kernel(
    q_ref, k_ref, v_ref, g_ref, o_ref, r_ref, e_ref, dq_ref, dk_ref, dv_ref, near_ref, t_ref
):
    lane = lax.broadcasted_iota(jnp.int32, (1, LANES), 1)
    low = lane < HD
    blocks = LENGTH // TILE
    block_of = lax.broadcasted_iota(jnp.int32, (LENGTH, LANES), 0) // TILE
    lanes = lax.broadcasted_iota(jnp.int32, (LENGTH, LANES), 1)
    q = q_ref[...]
    k = k_ref[...]
    v = v_ref[...]
    for hh in range(2):
        own = low if hh == 0 else ~low
        free = HD * (1 - hh)
        key = jnp.where(own, k, (lanes - free == block_of).astype(bf16))
        ones = jnp.where((lane == free) | (lane == free + 1), 1.0, 0.0).astype(bf16)
        value = jnp.where(own, v, ones)
        grad = jnp.where(own, g_ref[...].astype(f32) * r_ref[...], 0.0)
        term = -jnp.sum(grad * o_ref[...].astype(f32), axis=1, keepdims=True)
        grad = grad.astype(bf16)
        high = term.astype(bf16)
        rest = (term - high.astype(f32)).astype(bf16)
        joined = jnp.where(lane == free, high, jnp.where(lane == free + 1, rest, grad))
        shifted = e_ref[hh]
        ds = shifted * dot(joined, value, NT).astype(bf16)
        dq = dot(ds, key)
        t_ref[...] = jnp.zeros_like(t_ref)
        leftward = jnp.zeros((1, LANES), f32)
        rightward = jnp.zeros((1, LANES), f32)
        for a in range(blocks):
            first, last = max(a - 1, 0), min(a + 2, blocks)
            at = slice(a * TILE, (a + 1) * TILE)
            to = slice(TILE * (first - a + 1), TILE * (last - a + 1))
            t_ref[:, to] += ds[at, TILE * first : TILE * last].astype(f32)
            totals = jnp.sum(dq[at], axis=0, keepdims=True)
            block = lane - free
            leftward += jnp.where((block >= 0) & (block <= a - 2), totals, 0.0)
            rightward += jnp.where((block >= a + 2) & (block < blocks), totals, 0.0)
        dq = (dq * HD ** (-0.5)).astype(bf16)
        dv = dot(grad, shifted, TN).T.astype(bf16)
        dk = dot(q, ds, TN).T.astype(bf16)
        if hh == 0:
            dq_ref[...] = dq
            dk_ref[...] = dk
            dv_ref[...] = dv
        else:
            dq_ref[...] = jnp.where(low, dq_ref[...], dq)
            dk_ref[...] = jnp.where(low, dk_ref[...], dk)
            dv_ref[...] = jnp.where(low, dv_ref[...], dv)
        diagonals = jnp.concatenate([t_ref[...], jnp.zeros((TILE, TILE), f32)], axis=1)
        row = lax.broadcasted_iota(jnp.int32, (TILE, REACH), 0)
        for bit in range(7):
            moved = pltpu.roll(diagonals, REACH - (1 << bit), axis=1)
            diagonals = jnp.where(((row >> bit) & 1) == 1, moved, diagonals)
        at = lax.broadcasted_iota(jnp.int32, (1, REACH), 1)
        near_ref[0, hh : hh + 1, :] = (
            jnp.sum(diagonals, axis=0, keepdims=True)
            + jnp.where(at == 3 * TILE + 16, jnp.sum(leftward, axis=1, keepdims=True), 0.0)
            + jnp.where(at == 3 * TILE - 1, jnp.sum(rightward, axis=1, keepdims=True), 0.0)
        )


def attend_back(qkv, grad, heads, inverse, shifted, first, pairs):
    every = D // LANES
    part = lambda at: pl.BlockSpec((LENGTH, LANES), lambda p, at=at: (0, at * every + first + p))
    out = pl.BlockSpec((LENGTH, LANES), lambda p: (0, p))
    return pl.pallas_call(
        backward_kernel,
        grid=(pairs,),
        in_specs=[part(0), part(1), part(2), part(0), part(0), part(0)]
        + [pl.BlockSpec((2, LENGTH, LENGTH), lambda p: (first + p, 0, 0))],
        out_specs=[out, out, out]
        + [pl.BlockSpec((1, 2, REACH), lambda p: (p, 0, 0))],
        out_shape=[jax.ShapeDtypeStruct((LENGTH, pairs * LANES), bf16)] * 3
        + [jax.ShapeDtypeStruct((pairs, 2, REACH), f32)],
        scratch_shapes=[pltpu.VMEM((TILE, 3 * TILE), f32)],
        compiler_params=pltpu.CompilerParams(vmem_limit_bytes=VMEM_LIMIT),
        cost_estimate=pl.CostEstimate(
            flops=64 * pairs * LENGTH * LENGTH * HD,
            bytes_accessed=pairs * 6 * 2**20,
            transcendentals=0,
        ),
        name="attend_back",
    )(qkv, qkv, qkv, grad, heads, inverse, shifted)


def params():
    return pltpu.CompilerParams(vmem_limit_bytes=VMEM_LIMIT)


def cost(flops, megabytes):
    return pl.CostEstimate(flops=flops, bytes_accessed=megabytes * 2**20, transcendentals=0)


def put_rows(slot, first, count, rows):
    ids = first + lax.broadcasted_iota(jnp.int32, (count, 1), 0)
    return dot((slot == ids).astype(bf16), rows).astype(bf16)


def slots_kernel(routes_ref, capacity_ref, x_ref, sent_ref, wide_ref, split_ref, *, slots, block):
    step = pl.program_id(0)
    tokens = routes_ref.shape[1]
    experts = capacity_ref.shape[0]

    @pl.when(step == 0)
    def _():
        choice = routes_ref[...]
        chosen = choice == lax.broadcasted_iota(jnp.int32, (experts, 1), 0)
        before = (
            lax.broadcasted_iota(jnp.int32, (tokens, tokens), 0)
            < lax.broadcasted_iota(jnp.int32, (tokens, tokens), 1)
        ).astype(f32)
        counts = dot(chosen.astype(f32).astype(bf16), before.astype(bf16))
        place = jnp.sum(jnp.where(chosen, counts, 0.0), axis=0, keepdims=True).astype(jnp.int32)
        limit = jnp.zeros_like(choice)
        for e in range(experts):
            limit = jnp.where(choice == e, capacity_ref[e], limit)
        kept = place < limit
        chunk = slots // 2
        late = (place >= chunk).astype(jnp.int32)
        split = late * experts * chunk + choice * chunk + place - late * chunk
        wide_ref[...] = jnp.where(kept, choice * slots + place, -1)
        split_ref[...] = jnp.where(kept, split, -1)

    sent_ref[...] = put_rows(wide_ref[...], step * block, block, x_ref[...])


def place_rows(routes_row, capacity, rows, slots):
    tokens = rows.shape[0]
    total = capacity.shape[0] * slots
    block = total // 4
    row = pl.BlockSpec((1, tokens), lambda i: (0, 0))
    return pl.pallas_call(
        partial(slots_kernel, slots=slots, block=block),
        grid=(4,),
        in_specs=[
            row,
            pl.BlockSpec(memory_space=pltpu.SMEM),
            pl.BlockSpec((tokens, D), lambda i: (0, 0)),
        ],
        out_specs=[pl.BlockSpec((block, D), lambda i: (i, 0)), row, row],
        out_shape=[
            jax.ShapeDtypeStruct((total, D), bf16),
            jax.ShapeDtypeStruct((1, tokens), jnp.int32),
            jax.ShapeDtypeStruct((1, tokens), jnp.int32),
        ],
        compiler_params=params(),
        cost_estimate=cost(2 * total * tokens * D, 6),
        name="place_rows",
    )(routes_row, capacity, rows)


def later_kernel(slot_ref, x_ref, sent_ref, *, block, offset):
    first = offset + pl.program_id(0) * block
    sent_ref[...] = put_rows(slot_ref[...], first, block, x_ref[...])


def later_rows(split, rows):
    tokens = rows.shape[0]
    block = tokens // 2
    return pl.pallas_call(
        partial(later_kernel, block=block, offset=tokens),
        grid=(2,),
        in_specs=[
            pl.BlockSpec((1, tokens), lambda i: (0, 0)),
            pl.BlockSpec((tokens, D), lambda i: (0, 0)),
        ],
        out_specs=pl.BlockSpec((block, D), lambda i: (i, 0)),
        out_shape=jax.ShapeDtypeStruct((tokens, D), bf16),
        compiler_params=params(),
        cost_estimate=cost(2 * tokens * tokens * D, 3),
        name="later_rows",
    )(split, rows)


def sides(core, value):
    half = value.shape[1] // 2
    left, right = value[:, :half], value[:, half:]
    return jnp.where(core == 0, left, right), jnp.where(core == 0, right, left)


def joined(core, mine, other):
    return jnp.concatenate(
        [jnp.where(core == 0, mine, other), jnp.where(core == 0, other, mine)], axis=1
    )


def shuffle(order_ref, to_ref):
    source = lax.broadcasted_iota(jnp.int32, (D, 1), 0)
    to_ref[...] = (order_ref[...] == source).astype(bf16)


def project_kernel(
    core_ref, order_ref, gain_ref, x_ref, q0_ref, q1_ref, k0_ref, k1_ref, v0_ref, v1_ref,
    qkv_ref, mixed_ref, shuffle_ref,
):
    core = core_ref[0]

    @pl.when(pl.program_id(0) == 0)
    def _():
        shuffle(order_ref, shuffle_ref)

    x = x_ref[...].astype(f32)
    scale = lax.rsqrt(jnp.mean(x * x, axis=-1, keepdims=True) + epsilon)
    low = (x * scale * gain_ref[...]).astype(bf16)
    mixed_ref[...] = dot(low, shuffle_ref[...]).astype(bf16)
    mine, other = sides(core, low)
    pairs = [(q0_ref, q1_ref), (k0_ref, k1_ref), (v0_ref, v1_ref)]
    for at, (near, far) in enumerate(pairs):
        value = dot(mine, near[...]) + dot(other, far[...])
        value = value * HD ** (-0.5) if at == 0 else value
        qkv_ref[:, at * D : (at + 1) * D] = value.astype(bf16)


ROWS = 256
SMALL = pl.BlockSpec(memory_space=pltpu.SMEM)
VECTOR = pl.BlockSpec((1, D), lambda i: (0, 0))
BLOCK = pl.BlockSpec((ROWS, D), lambda i: (i, 0))
HALF = pl.BlockSpec((D // 2, D), lambda i: (0, 0))


def project(core, order, gain, x, weights):
    tokens = x.shape[0]
    return pl.pallas_call(
        project_kernel,
        grid=(tokens // ROWS,),
        in_specs=[SMALL, VECTOR, VECTOR, BLOCK] + [HALF] * 6,
        out_specs=[pl.BlockSpec((ROWS, 3 * D), lambda i: (i, 0)), BLOCK],
        out_shape=[
            jax.ShapeDtypeStruct((tokens, 3 * D), bf16),
            jax.ShapeDtypeStruct((tokens, D), bf16),
        ],
        scratch_shapes=[pltpu.VMEM((D, D), bf16)],
        compiler_params=params(),
        cost_estimate=cost(8 * tokens * D * D, 12),
        name="project",
    )(core, order, gain, x, *weights)


def hidden_kernel(
    core_ref, order_ref, gain_ref, slot_ref, x_ref, heads_ref, o0_ref, o1_ref,
    hidden_ref, mixed_ref, low_ref, sent_ref, shuffle_ref, *, blocks,
):
    step = pl.program_id(0)
    core = core_ref[0]

    @pl.when(step == 0)
    def _():
        shuffle(order_ref, shuffle_ref)

    @pl.when(step < blocks)
    def _():
        heads = heads_ref[...]
        mixed_ref[...] = dot(heads, shuffle_ref[...]).astype(bf16)
        mine, other = sides(core, heads)
        hidden = x_ref[...].astype(f32) + dot(mine, o0_ref[...]) + dot(other, o1_ref[...])
        scale = lax.rsqrt(jnp.mean(hidden * hidden, axis=-1, keepdims=True) + epsilon)
        hidden_ref[...] = hidden
        at = pl.multiple_of(step * ROWS, ROWS)
        low_ref[pl.ds(at, ROWS), :] = (hidden * scale * gain_ref[...]).astype(bf16)

    @pl.when(step >= blocks)
    def _():
        count = sent_ref.shape[0]
        sent_ref[...] = put_rows(slot_ref[...], (step - blocks) * count, count, low_ref[...])


def make_hidden(core, order, gain, split, x, heads, near, far):
    tokens = x.shape[0]
    blocks = tokens // ROWS
    held = pl.BlockSpec((ROWS, D), lambda i: (jnp.minimum(i, blocks - 1), 0))
    return pl.pallas_call(
        partial(hidden_kernel, blocks=blocks),
        grid=(blocks + 2,),
        in_specs=[SMALL, VECTOR, VECTOR, pl.BlockSpec((1, tokens), lambda i: (0, 0))]
        + [held, held, HALF, HALF],
        out_specs=[
            held,
            held,
            pl.BlockSpec((tokens, D), lambda i: (0, 0)),
            pl.BlockSpec((tokens // 2, D), lambda i: (jnp.maximum(i - blocks, 0), 0)),
        ],
        out_shape=[
            jax.ShapeDtypeStruct((tokens, D), f32),
            jax.ShapeDtypeStruct((tokens, D), bf16),
            jax.ShapeDtypeStruct((tokens, D), bf16),
            jax.ShapeDtypeStruct((tokens, D), bf16),
        ],
        scratch_shapes=[pltpu.VMEM((D, D), bf16)],
        compiler_params=params(),
        cost_estimate=cost(8 * tokens * D * D, 12),
        name="make_hidden",
    )(core, order, gain, split, x, heads, near, far)


def take_rows(slot, total, rows):
    ids = lax.broadcasted_iota(jnp.int32, (1, total), 1)
    return dot((slot == ids).astype(bf16), rows)


def hidden_back_kernel(
    core_ref, gain_ref, slot_ref, back0_ref, back1_ref, cot_ref, hidden_ref, o0_ref, o1_ref,
    grad_ref, branch_ref, heads_ref, term_ref,
):
    core = core_ref[0]
    slot = slot_ref[...]
    total = back0_ref.shape[0]
    hidden = hidden_ref[...]
    grad_ffn = take_rows(slot, total, back0_ref[...]) + take_rows(
        slot - total, total, back1_ref[...]
    )
    scale = lax.rsqrt(jnp.mean(hidden * hidden, axis=-1, keepdims=True) + epsilon)
    weighted = gain_ref[...] * grad_ffn
    along = jnp.mean(weighted * hidden, axis=-1, keepdims=True)
    grad = cot_ref[...].astype(f32) + scale * weighted - hidden * (scale * scale * scale * along)
    branch = grad.astype(bf16)
    grad_ref[...] = grad
    branch_ref[...] = branch
    heads = joined(core, dot(branch, o0_ref[...], NT), dot(branch, o1_ref[...], NT))
    heads_ref[...] = heads.astype(bf16)
    term = jnp.sum(grad_ffn * hidden * scale, axis=0, keepdims=True)

    @pl.when(pl.program_id(0) == 0)
    def _():
        term_ref[...] = jnp.zeros_like(term_ref)

    term_ref[...] += term


def hidden_back(core, gain, slot, back0, back1, cot, hidden, near, far):
    tokens = cot.shape[0]
    every = pl.BlockSpec((tokens, D), lambda i: (0, 0))
    return pl.pallas_call(
        hidden_back_kernel,
        grid=(tokens // ROWS,),
        in_specs=[SMALL, VECTOR, pl.BlockSpec((ROWS, 1), lambda i: (i, 0)), every, every]
        + [BLOCK, BLOCK, HALF, HALF],
        out_specs=[BLOCK, BLOCK, BLOCK, VECTOR],
        out_shape=[
            jax.ShapeDtypeStruct((tokens, D), f32),
            jax.ShapeDtypeStruct((tokens, D), bf16),
            jax.ShapeDtypeStruct((tokens, D), bf16),
            jax.ShapeDtypeStruct((1, D), f32),
        ],
        compiler_params=params(),
        cost_estimate=cost(4 * tokens * tokens * D + 2 * tokens * D * D, 18),
        name="hidden_back",
    )(core, gain, slot, back0, back1, cot, hidden, near, far)


def input_back_kernel(
    core_ref, gain_ref, dq_ref, dk_ref, dv_ref, x_ref, grad_ref,
    q0_ref, q1_ref, k0_ref, k1_ref, v0_ref, v1_ref, out_ref, term_ref,
):
    core = core_ref[0]
    grads = [dq_ref[...], dk_ref[...], dv_ref[...]]
    mine = sum(dot(g, w[...], NT) for g, w in zip(grads, [q0_ref, k0_ref, v0_ref]))
    other = sum(dot(g, w[...], NT) for g, w in zip(grads, [q1_ref, k1_ref, v1_ref]))
    grad_attn = joined(core, mine, other)
    x = x_ref[...].astype(f32)
    scale = lax.rsqrt(jnp.mean(x * x, axis=-1, keepdims=True) + epsilon)
    weighted = gain_ref[...] * grad_attn
    along = jnp.mean(weighted * x, axis=-1, keepdims=True)
    out = grad_ref[...] + scale * weighted - x * (scale * scale * scale * along)
    out_ref[...] = out.astype(bf16)
    term = jnp.sum(grad_attn * x * scale, axis=0, keepdims=True)

    @pl.when(pl.program_id(0) == 0)
    def _():
        term_ref[...] = jnp.zeros_like(term_ref)

    term_ref[...] += term


def input_back(core, gain, grads, x, grad, weights):
    tokens = x.shape[0]
    return pl.pallas_call(
        input_back_kernel,
        grid=(tokens // ROWS,),
        in_specs=[SMALL, VECTOR] + [BLOCK] * 5 + [HALF] * 6,
        out_specs=[BLOCK, VECTOR],
        out_shape=[
            jax.ShapeDtypeStruct((tokens, D), bf16),
            jax.ShapeDtypeStruct((1, D), f32),
        ],
        compiler_params=params(),
        cost_estimate=cost(6 * tokens * D * D, 16),
        name="input_back",
    )(core, gain, *grads, x, grad, *weights)


def output_kernel(slot_ref, rows_ref, hidden_ref, out_ref):
    produced = take_rows(slot_ref[...], rows_ref.shape[0], rows_ref[...])
    out_ref[...] = (hidden_ref[...] + produced).astype(bf16)


def make_output(slot, rows, hidden):
    tokens = hidden.shape[0]
    return pl.pallas_call(
        output_kernel,
        grid=(tokens // ROWS,),
        in_specs=[
            pl.BlockSpec((ROWS, 1), lambda i: (i, 0)),
            pl.BlockSpec(rows.shape, lambda i: (0, 0)),
            BLOCK,
        ],
        out_specs=BLOCK,
        out_shape=jax.ShapeDtypeStruct((tokens, D), bf16),
        compiler_params=params(),
        cost_estimate=cost(2 * rows.shape[0] * tokens * D, 9),
        name="make_output",
    )(slot, rows, hidden)


def expert_kernel(
    me_ref, rows_ref, cot_ref, router_ref, up0_ref, up1_ref, down0_ref, down1_ref,
    sent_ref, back_ref, gp_ref, gl_ref, act_ref, gb_ref,
    out_ref, grow_ref, p_ref, gate_ref, *, experts, steps,
):
    step = pl.program_id(0)
    me = me_ref[0]
    lane = lax.broadcasted_iota(jnp.int32, (1, LANES), 1)

    @pl.when(step == 0)
    def _():
        logits = dot(rows_ref[...], router_ref[...])
        logits = jnp.where(lane < experts, logits, -1e30)
        weight = jnp.exp(logits - jnp.max(logits, axis=1, keepdims=True))
        p = weight / jnp.sum(weight, axis=1, keepdims=True)
        gate = experts * jnp.sum(jnp.where(lane == me, p, 0.0), axis=1, keepdims=True)
        p_ref[...] = p
        gate_ref[...] = gate
        gp_ref[...] = (gate * cot_ref[...].astype(f32)).astype(bf16)
        out_ref[...] = jnp.zeros_like(out_ref)
        grow_ref[...] = jnp.zeros_like(grow_ref)

    mine = step < steps // 2
    up = jnp.where(mine, up0_ref[...], up1_ref[...])
    down = jnp.where(mine, down0_ref[...], down1_ref[...])
    v = dot(rows_ref[...], up)
    scale = np.sqrt(2 / np.pi).astype(np.float32)
    square = v * v
    tanh = jnp.tanh(scale * v * (1.0 + 0.044715 * square))
    half = 0.5 + 0.5 * tanh
    act = (v * half).astype(bf16)
    slope = half + (0.5 * scale) * v * (1.0 - tanh * tanh) * (1.0 + (3 * 0.044715) * square)
    gb = (slope * dot(gp_ref[...], down, NT)).astype(bf16)
    act_ref[0] = act
    gb_ref[0] = gb
    out_ref[...] += dot(act, down)
    grow_ref[...] += dot(gb, up, NT)

    @pl.when(step == steps - 1)
    def _():
        gate = gate_ref[...]
        produced = out_ref[...]
        sent_ref[...] = (gate * produced).astype(bf16)
        grad_gate = jnp.sum(produced * cot_ref[...].astype(f32), axis=1, keepdims=True)
        chosen = jnp.where(lane == me, 1.0, 0.0)
        grad_logits = (grad_gate * gate * (chosen - p_ref[...])).astype(bf16)
        gl_ref[...] = grad_logits
        back_ref[...] = (grow_ref[...] + dot(grad_logits, router_ref[...], NT)).astype(bf16)


def expert_part(me, rows, cot, router, up0, up1, down0, down1, experts):
    count = rows.shape[0]
    half = up0.shape[1]
    tile = 512
    each = half // tile
    steps = 2 * each
    whole = pl.BlockSpec((count, D), lambda f: (0, 0))
    narrow = pl.BlockSpec((count, LANES), lambda f: (0, 0))
    near = lambda f: jnp.minimum(f, each - 1)
    later = lambda f: jnp.maximum(f - each, 0)
    wide = pl.BlockSpec((1, count, tile), lambda f: (f // each, 0, f % each))
    return pl.pallas_call(
        partial(expert_kernel, experts=experts, steps=steps),
        grid=(steps,),
        in_specs=[
            pl.BlockSpec(memory_space=pltpu.SMEM),
            whole,
            whole,
            pl.BlockSpec((D, LANES), lambda f: (0, 0)),
            pl.BlockSpec((D, tile), lambda f: (0, near(f))),
            pl.BlockSpec((D, tile), lambda f: (0, later(f))),
            pl.BlockSpec((tile, D), lambda f: (near(f), 0)),
            pl.BlockSpec((tile, D), lambda f: (later(f), 0)),
        ],
        out_specs=[whole, whole, whole, narrow, wide, wide],
        out_shape=[
            jax.ShapeDtypeStruct((count, D), bf16),
            jax.ShapeDtypeStruct((count, D), bf16),
            jax.ShapeDtypeStruct((count, D), bf16),
            jax.ShapeDtypeStruct((count, LANES), bf16),
            jax.ShapeDtypeStruct((2, count, half), bf16),
            jax.ShapeDtypeStruct((2, count, half), bf16),
        ],
        scratch_shapes=[
            pltpu.VMEM((count, D), f32),
            pltpu.VMEM((count, D), f32),
            pltpu.VMEM((count, LANES), f32),
            pltpu.VMEM((count, 1), f32),
        ],
        compiler_params=pltpu.CompilerParams(vmem_limit_bytes=44 * 2**20),
        cost_estimate=pl.CostEstimate(
            flops=16 * count * D * half,
            bytes_accessed=30 * 2**20,
            transcendentals=2 * count * half,
        ),
        name="expert_part",
    )(me, rows, cot, router, up0, up1, down0, down1)


def terms_kernel(attn_ref, heads_ref, *refs):
    near_refs, far_refs = refs[4:6], refs[6:8]
    step = pl.program_id(0)
    half = D // 2
    for at in range(4):

        @pl.when(step == at)
        def _(at=at):
            left = attn_ref if at < 3 else heads_ref
            total = dot(left[...], refs[at][...], TN).astype(bf16)
            near_refs[at // 2][...] = total[:half]
            far_refs[at // 2][...] = total[half:]


def weight_terms(attn, heads, grads):
    tokens = attn.shape[0]
    whole = pl.BlockSpec((tokens, D), lambda i: (0, 0))
    early = pl.BlockSpec((D // 2, D), lambda i: (0, jnp.minimum(i, 1)))
    late = pl.BlockSpec((D // 2, D), lambda i: (0, jnp.maximum(i - 2, 0)))
    return pl.pallas_call(
        terms_kernel,
        grid=(4,),
        in_specs=[whole] * 6,
        out_specs=[early, late, early, late],
        out_shape=[jax.ShapeDtypeStruct((D // 2, 2 * D), bf16)] * 4,
        compiler_params=params(),
        cost_estimate=cost(8 * tokens * D * D, 14),
        name="weight_terms",
    )(attn, heads, *grads)


def up_kernel(*refs):
    rows, gbs = refs[0:2], refs[2:4]
    total = sum(dot(r[...], g[0], TN) for r, g in zip(rows, gbs))
    for received in refs[4:-1]:
        total = total + received[...].astype(f32)
    refs[-1][...] = total.astype(refs[-1].dtype)


def down_kernel(*refs):
    gps, acts = refs[0:2], refs[2:4]
    total = sum(dot(a[0], g[...], TN) for g, a in zip(gps, acts))
    for received in refs[4:-1]:
        total = total + received[...].astype(f32)
    refs[-1][...] = total.astype(refs[-1].dtype)


def weight_sum(kernel, half, narrow, wide, received, name, kind=f32):
    count = narrow[0].shape[0]
    width = wide[0].shape[2]
    tile = 512
    if kernel is up_kernel:
        out = pl.BlockSpec((D, tile), lambda f: (0, f))
        shape = (D, width)
    else:
        out = pl.BlockSpec((tile, D), lambda f: (f, 0))
        shape = (width, D)
    return pl.pallas_call(
        kernel,
        grid=(width // tile,),
        in_specs=[pl.BlockSpec((count, D), lambda f: (0, 0))] * 2
        + [pl.BlockSpec((1, count, tile), lambda f: (half, 0, f))] * 2
        + [out] * len(received),
        out_specs=out,
        out_shape=jax.ShapeDtypeStruct(shape, kind),
        compiler_params=params(),
        cost_estimate=cost(4 * count * D * width, 16),
        name=name,
    )(*narrow, *wide, *received)


def shards(
    tokens,
    segments,
    routes,
    capacity,
    first_gain,
    query_weight,
    key_weight,
    value_weight,
    output_weight,
    position_bias,
    second_gain,
    router_weight,
    expert_up,
    expert_down,
    cotangent,
):
    owners = lax.axis_size("expert")
    cores = lax.axis_size("dp")
    core = lax.axis_index("dp")
    expert = lax.axis_index("expert")
    token_count = tokens.shape[0]
    experts = capacity.shape[0]
    slots = 2 * token_count // experts
    chunk = slots // 2
    share = D // cores // owners
    bits = owners.bit_length() - 1
    core_at = core.reshape(1).astype(jnp.int32)
    me = expert.reshape(1).astype(jnp.int32)

    def other_core(value):
        return lax.ppermute(value, "dp", [(i, i ^ 1) for i in range(cores)])

    def partner(value, bit):
        return lax.ppermute(value, "expert", [(i, i ^ (1 << bit)) for i in range(owners)])

    def both(mine, other):
        return jnp.where(
            core == 0,
            jnp.concatenate([mine, other], axis=0),
            jnp.concatenate([other, mine], axis=0),
        )

    def exchange(value):
        shape = (experts, -1, D)
        return lax.all_to_all(
            value.reshape(shape), "expert", split_axis=0, concat_axis=0, tiled=True
        )

    cot_sent, wide, split = place_rows(
        routes.reshape(1, token_count), capacity, cotangent, slots
    )
    cot_arrived = exchange(cot_sent)
    wide_column = wide.reshape(token_count, 1)
    split_column = split.reshape(token_count, 1)

    small = jnp.concatenate(
        [
            router_weight,
            first_gain[:, None],
            second_gain[:, None],
            jnp.zeros((D // cores, LANES - 2), bf16),
        ],
        axis=1,
    )
    small_full = both(small, other_core(small))
    bias_full = both(position_bias, other_core(position_bias)).astype(f32)
    mixer = []
    for weight in (query_weight, key_weight, value_weight):
        mixer += [weight, other_core(weight)]
    output_far = other_core(output_weight)
    up0 = expert_up[0]
    down0 = expert_down[0]
    up1 = other_core(up0)
    down1 = other_core(down0)
    router = small_full[:, :experts]
    gains = small_full[:, experts : experts + 2].astype(f32).T
    first_full = gains[0:1]
    second_full = gains[1:2]
    router_wide = jnp.pad(router, ((0, 0), (0, LANES - experts)))

    order = np.arange(D).reshape((cores,) + (2,) * bits + (share,))
    order = order.transpose((0,) + tuple(range(bits, 0, -1)) + (bits + 1,)).reshape(cores, -1)
    order = jnp.where(core == 0, order.reshape(1, D), order[::-1].reshape(1, D)).astype(jnp.int32)

    qkv, attn_mixed = project(core_at, order, first_full, tokens, mixer)
    near = np.clip(np.arange(REACH) - REACH // 2, 1 - LENGTH, LENGTH - 1)
    bias = jnp.dot(jnp.asarray(bucket_onehot(near)), bias_full, precision=lax.Precision.HIGHEST)
    bias = bias.T.reshape(H // 2, 2, REACH)
    marks = segments.astype(f32)
    heads_low, shifted, inverse = attend(bias, marks[:, None], marks[None, :], qkv)
    hidden, heads_mixed, ffn_low, sent0 = make_hidden(
        core_at, order, second_full, split, tokens, heads_low, output_weight, output_far
    )

    rows0 = exchange(sent0).reshape(token_count, D)
    cot_rows = [
        cot_arrived[:, c * chunk : (c + 1) * chunk].reshape(experts * chunk, D) for c in range(2)
    ]
    sent1, rows0 = lax.optimization_barrier((later_rows(split, ffn_low), rows0))
    rows1 = exchange(sent1).reshape(token_count, D)
    arrived = [rows0, rows1]
    parts = [
        expert_part(me, arrived[c], cot_rows[c], router_wide, up0, up1, down0, down1, experts)
        for c in range(2)
    ]
    back0 = exchange(parts[0][1]).reshape(token_count, D)
    back_sent1, back0 = lax.optimization_barrier((parts[1][1], back0))
    back1 = exchange(back_sent1).reshape(token_count, D)

    gps = [part[2] for part in parts]
    acts = [part[4] for part in parts]
    gbs = [part[5] for part in parts]
    weight_sent = [
        weight_sum(up_kernel, 1, arrived, gbs, [], "up_sent", bf16),
        weight_sum(down_kernel, 1, gps, acts, [], "down_sent", bf16),
        weight_sum(up_kernel, 0, arrived, gbs, [], "up_own"),
    ]
    router_term = sum(dot(r, part[3], TN) for r, part in zip(arrived, parts))[:, :experts]
    out_sent = jnp.concatenate(
        [part[0].reshape(experts, chunk, D) for part in parts], axis=1
    )

    out_sent, back0, back1, *weight_sent = lax.optimization_barrier(
        (out_sent, back0, back1, *weight_sent)
    )
    out_rows = exchange(out_sent).reshape(experts * slots, D)
    weight_received = [other_core(value) for value in weight_sent[:2]]
    grad_hidden, grad_branch, grad_heads, second_term = hidden_back(
        core_at, second_full, split_column, back0, back1, cotangent, hidden, output_weight, output_far
    )
    dq, dk, dv, near_sums = attend_back(
        qkv, grad_heads, heads_low, inverse, shifted, 0, H // 2
    )
    grads = [dq, dk, dv]

    input_grad, first_term = input_back(core_at, first_full, grads, tokens, grad_hidden, mixer)

    offsets = np.arange(REACH)
    offsets = np.where(offsets < 3 * TILE, offsets - TILE, offsets - TILE - REACH)
    bias_term = jnp.dot(
        jnp.asarray(bucket_onehot(offsets).T),
        near_sums.reshape(H, REACH).T,
        precision=lax.Precision.HIGHEST,
    )
    sizes = [D * experts, D, D, BUCKETS * H]
    totals = jnp.concatenate(
        [part.reshape(-1) for part in (router_term, second_term, first_term, bias_term)]
    ).reshape(-1, LANES)
    totals = totals + other_core(totals)
    dq, first_term = lax.optimization_barrier((dq, first_term))
    grads = [dq, dk, dv]
    *pieces, far0, far1 = weight_terms(attn_mixed, heads_mixed, [*grads, grad_branch])
    received = [other_core(far0), other_core(far1)]
    *received, totals, out_rows = lax.optimization_barrier((*received, totals, out_rows))
    pieces = [
        (near.astype(f32) + far.astype(f32)).astype(bf16) for near, far in zip(pieces, received)
    ]
    for step in range(bits):
        if step == 0:
            acts[0], out_rows = lax.optimization_barrier((acts[0], out_rows))
            down_grad = weight_sum(down_kernel, 0, gps, acts, weight_received[1:], "down_sum")
        if step == 1:
            pieces[0], out_rows = lax.optimization_barrier((pieces[0], out_rows))
            layer_out = make_output(wide_column, out_rows, hidden)
        if step == 2:
            pieces[0], up_own = lax.optimization_barrier((pieces[0], weight_sent[2]))
            up_grad = up_own + weight_received[0].astype(f32)
        if step == 2:
            pieces = [jnp.concatenate(pieces, axis=1)]
        for at in range(len(pieces)):
            bit = step ^ 1 if at == 1 else step
            cut = 1 if at == 1 and step == 0 else 0
            piece = pieces[at]
            rows, columns = piece.shape
            piece = piece.reshape(1 << cut, 2, rows >> (cut + 1), columns)
            upper = ((expert >> bit) & 1) == 1
            kept = jnp.where(upper, piece[:, 1], piece[:, 0]).reshape(-1, columns)
            sent = jnp.where(upper, piece[:, 0], piece[:, 1]).reshape(-1, columns)
            kept = kept.astype(f32) + partner(sent, bit).astype(f32)
            pieces[at] = kept if step == bits - 1 else kept.astype(bf16)
        totals = totals + partner(totals, step)
        *pieces, totals = lax.optimization_barrier((*pieces, totals))
    query_grad, key_grad, value_grad, output_grad = jnp.split(pieces[0], 4, axis=1)

    totals = jnp.split(totals.reshape(-1), np.cumsum(sizes)[:-1])
    first_row = (core * owners + expert) * share
    own = lambda value: lax.dynamic_slice_in_dim(value, first_row, share, axis=0)
    router_grad = own(totals[0].reshape(D, experts))
    second_grad = own(totals[1])
    first_grad = own(totals[2])
    bias_grad = totals[3].reshape(BUCKETS, H)
    return (
        layer_out,
        input_grad,
        first_grad,
        query_grad,
        key_grad,
        value_grad,
        output_grad,
        bias_grad,
        second_grad,
        router_grad,
        up_grad[None],
        down_grad[None],
    )


def solution(mesh):
    both = ("dp", "expert")
    placed = (
        P(both, None),
        P(both),
        P(both, None),
        P(),
        P("dp"),
        P("dp", None),
        P("dp", None),
        P("dp", None),
        P("dp", None),
        P("dp", None),
        P("dp"),
        P("dp", None),
        P("expert", None, "dp"),
        P("expert", "dp", None),
        P(both, None),
    )
    return jax.shard_map(
        shards,
        mesh=mesh,
        in_specs=placed,
        out_specs=(
            P(both, None),
            P(both, None),
            P(both),
            P(both, None),
            P(both, None),
            P(both, None),
            P(both, None),
            P(),
            P(both),
            P(both, None),
            P("expert", None, "dp"),
            P("expert", "dp", None),
        ),
        check_vma=False,
    )
```
